256 devices in a mesh: grp: 8 (over z), tile: 32 (over x, y, core).
Axes of the slice: x: 4, y: 4, z: 8, core: 2. Of those that a mesh axis runs over, the one named last changes fastest.
Arguments:
- speed: float32 [128, 2, 32, 128], P('tile'), may hold values from 0.15 to 0.4
- density: float32 [128, 2, 32, 128], P('tile'), may hold values from 1 to 3
- fwd_state: bfloat16 [256, 4, 32, 32, 128], P(('grp', 'tile')), may hold values from -6 to 6
- adj_state: bfloat16 [256, 4, 32, 32, 128], P(('grp', 'tile')), may hold values from -6 to 6
- aperture: int32 [256, 16], P(('grp', 'tile')), may hold values from 0 to 127, as said below
- src_pos: int32 [256, 3], P(('grp', 'tile')), may hold values from 0 to 127, as said below
- wavelet: float32 [256, 4], P(('grp', 'tile')), may hold values from -15 to 15
- rec_pos: int32 [256, 32, 2], P(('grp', 'tile')), may hold values from 0 to 127, as said below
- residual: float32 [256, 4, 32], P(('grp', 'tile')), may hold values from -6 to 6
Outputs:
- grad_speed: float32 [128, 2, 32, 128], P('tile')
- grad_density: float32 [128, 2, 32, 128], P('tile')
The draws below stay inside these ranges and needn't reach their ends.
Inputs may be any that keep to these rules, and one draw needn't show every extreme that they name: `aperture`: row s is (c + j) * 4 + e for j = 0 .. 15, with one c in 0 .. 16 and one e in 0 .. 3 for each shot, so a shot takes exactly one tile from each of 16 owners. `src_pos`: columns are x in 0 .. 31, y in 0 .. 31, z in 0 .. 127. `rec_pos`: columns are y in 0 .. 31 and z in 0 .. 127.
All inputs are finite; a program needn't handle non-finite values.
Results may differ from the reference program's by a relative error of at most 0.0003.
Values sent between devices are 32-bit elements; how exact they have to be, the bound alone decides.
A program may use at most 64 MiB of HBM per device.

```python
import math
import jax
import jax.numpy as jnp
from jax import lax

TX = 2
TY = 32
NZ = 128
TPD = 4
STEPS = 4
AX = 16
APX = 32
APY = 32
NREC = 32
NTILES = 128
SHOTS = 256
N_TILE = 32


def draw_aperture(key, part):
    corner_key, depth_key = jax.random.split(jax.random.fold_in(key, 11))
    corner = jax.random.randint(corner_key, (SHOTS, 1), 0, N_TILE - AX + 1)
    column = jax.random.randint(depth_key, (SHOTS, 1), 0, TPD)
    stripes = corner + jnp.arange(AX, dtype=jnp.int32)[None, :]
    return (stripes * TPD + column).astype(jnp.int32)


def draw_src_pos(key, part):
    upper = jnp.array([APX, APY, NZ], dtype=jnp.int32)
    return jax.random.randint(jax.random.fold_in(key, 23), (SHOTS, 3), 0, upper[None, :]).astype(jnp.int32)


def draw_rec_pos(key, part):
    upper = jnp.array([APY, NZ], dtype=jnp.int32)
    return jax.random.randint(jax.random.fold_in(key, 37), (SHOTS, NREC, 2), 0, upper[None, None, :]).astype(jnp.int32)


def block_scale(stream_key, dims, cuts, low, largest):
    loudness, own = 1.0, jax.random.fold_in(stream_key, 6)
    for position, blocks in cuts:
        draws = jnp.exp(jax.random.uniform(jax.random.fold_in(own, position), (blocks,), jnp.float32, low / len(cuts), largest / len(cuts)))
        loudness = loudness * jnp.repeat(draws, dims[position] // blocks).reshape([-1 if axis == position else 1 for axis in range(len(dims))])
    return loudness


def bell_draw(rng, shape, deviation, bound, cuts=(), kind=jnp.bfloat16):
    values = deviation * jax.random.normal(rng, shape, jnp.float32)
    if cuts:
        values = values * block_scale(rng, shape, cuts, -0.22, 0.18)
    return jnp.clip(values, -bound, bound).astype(kind)


def setup_inputs(seed: int = 0) -> dict:
    splits = jax.random.split(jax.random.key(seed), 10)
    return {
        "speed": jnp.clip(0.15 + 0.25 * jax.random.uniform(splits[0], (NTILES, TX, TY, NZ), jnp.float32) ** block_scale(splits[0], (NTILES, TX, TY, NZ), ((0, 32),), -0.2, 0.2), 0.15, 0.4),
        "density": jnp.clip(1.0 + 2.0 * jax.random.uniform(splits[1], (NTILES, TX, TY, NZ), jnp.float32) ** block_scale(splits[1], (NTILES, TX, TY, NZ), ((0, 32),), -0.2, 0.2), 1.0, 3.0),
        "fwd_state": bell_draw(splits[2], (SHOTS, 4, APX, APY, NZ), 1.0, 6.0, ((0, 256),)),
        "adj_state": bell_draw(splits[3], (SHOTS, 4, APX, APY, NZ), 1.0, 6.0, ((0, 256),)),
        "aperture": draw_aperture(jax.random.fold_in(splits[9], 71), 0),
        "src_pos": draw_src_pos(jax.random.fold_in(splits[9], 71), 0),
        "wavelet": bell_draw(splits[6], (SHOTS, STEPS), 3.0, 15.0, ((0, 256),), jnp.float32),
        "rec_pos": draw_rec_pos(jax.random.fold_in(splits[9], 71), 0),
        "residual": bell_draw(splits[8], (SHOTS, STEPS, NREC), 1.0, 6.0, ((0, 256),), jnp.float32),
    }


COEF = (1225.0 / 1024.0, -245.0 / 3072.0, 49.0 / 5120.0, -5.0 / 7168.0)

def padded_along(values, which_dim):
    widths = [(0, 0), (0, 0), (0, 0)]
    widths[which_dim] = (4, 4)
    return jnp.pad(values, widths)

def forward_diff(values, which_dim):
    length = values.shape[which_dim]
    padded = padded_along(values, which_dim)
    total = jnp.zeros_like(values)
    for order in range(1, 5):
        upper = lax.slice_in_dim(padded, 4 + order, 4 + order + length, axis=which_dim)
        lower = lax.slice_in_dim(padded, 5 - order, 5 - order + length, axis=which_dim)
        total = total + COEF[order - 1] * (upper - lower)
    return total

def backward_diff(values, which_dim):
    length = values.shape[which_dim]
    padded = padded_along(values, which_dim)
    total = jnp.zeros_like(values)
    for order in range(1, 5):
        upper = lax.slice_in_dim(padded, 3 + order, 3 + order + length, axis=which_dim)
        lower = lax.slice_in_dim(padded, 4 - order, 4 - order + length, axis=which_dim)
        total = total + COEF[order - 1] * (upper - lower)
    return total

def advance(pressure, velocity, bulk, buoyancy, source):
    moved = tuple((velocity[which_dim] + buoyancy * forward_diff(pressure, which_dim) for which_dim in range(3)))
    divergence = backward_diff(moved[0], 0) + backward_diff(moved[1], 1) + backward_diff(moved[2], 2)
    return (pressure + bulk * divergence + source, moved)

def evolve(speed_ap, density_ap, fwd_state, adj_state, src_pos, wavelet, rec_pos, residual):
    bulk = density_ap * speed_ap * speed_ap
    buoyancy = 1.0 / density_ap
    xs_cells = jnp.arange(speed_ap.shape[0], dtype=jnp.int32)
    ys_cells = jnp.arange(speed_ap.shape[1], dtype=jnp.int32)
    zs_cells = jnp.arange(speed_ap.shape[2], dtype=jnp.int32)
    src_mask = ((xs_cells == src_pos[0])[:, None, None] & (ys_cells == src_pos[1])[None, :, None] & (zs_cells == src_pos[2])[None, None, :]).astype(jnp.float32)
    rec_mask = ((ys_cells[None, :, None] == rec_pos[:, 0][:, None, None]) & (zs_cells[None, None, :] == rec_pos[:, 1][:, None, None])).astype(jnp.float32)
    state = fwd_state.astype(jnp.float32)
    pressure = state[0]
    velocity = (state[1], state[2], state[3])
    changes = []
    steps_count = wavelet.shape[0]
    for step_index in range(steps_count):
        new_pressure, new_velocity = advance(pressure, velocity, bulk, buoyancy, wavelet[step_index] * src_mask)
        changes.append((new_pressure - pressure, tuple((new_velocity[d] - velocity[d] for d in range(3)))))
        pressure, velocity = (new_pressure, new_velocity)
    adjoint = adj_state.astype(jnp.float32)
    adj_pressure = adjoint[0]
    adj_velocity = (adjoint[1], adjoint[2], adjoint[3])
    bulk_image = jnp.zeros_like(bulk)
    buoy_image = jnp.zeros_like(bulk)
    for step_index in reversed(range(steps_count)):
        adj_pressure, adj_velocity = advance(adj_pressure, adj_velocity, bulk, buoyancy, residual[step_index][:, None, None] * rec_mask)
        bulk_image = bulk_image + changes[step_index][0] * adj_pressure
        dvel = changes[step_index][1]
        buoy_image = buoy_image + dvel[0] * adj_velocity[0] + dvel[1] * adj_velocity[1] + dvel[2] * adj_velocity[2]
    return (bulk_image, buoy_image)

def reference(speed, density, fwd_state, adj_state, aperture, src_pos, wavelet, rec_pos, residual):

    def one_shot(carry, inputs):
        fwd_one, adj_one, tiles_one, src_one, wave_one, recs_one, resid_one = inputs
        speed_ap = speed[tiles_one].reshape(AX * TX, TY, NZ)
        density_ap = density[tiles_one].reshape(AX * TX, TY, NZ)
        bulk_image, buoy_image = evolve(speed_ap, density_ap, fwd_one, adj_one, src_one, wave_one, recs_one, resid_one)
        bulk_acc = carry[0].at[tiles_one].add(bulk_image.reshape(AX, TX, TY, NZ))
        buoy_acc = carry[1].at[tiles_one].add(buoy_image.reshape(AX, TX, TY, NZ))
        return ((bulk_acc, buoy_acc), None)
    zeros = jnp.zeros(speed.shape, jnp.float32)
    (bulk_sum, buoy_sum), _ = lax.scan(one_shot, (zeros, zeros), (fwd_state, adj_state, aperture, src_pos, wavelet, rec_pos, residual))
    scale = 1.0 / math.sqrt(SHOTS)
    grad_speed = scale * (bulk_sum * (2.0 * density * speed))
    grad_density = scale * (bulk_sum * (speed * speed) - buoy_sum / (density * density))
    return (grad_speed, grad_density)
```

```python
import math

import jax
import jax.numpy as jnp
import numpy as np
from jax import lax
from jax.experimental import pallas as pl
from jax.experimental.pallas import tpu as pltpu
from jax.sharding import PartitionSpec as P

COEF = (1225.0 / 1024.0, -245.0 / 3072.0, 49.0 / 5120.0, -5.0 / 7168.0)
SCALE = COEF[0] / (165.0 / 128.0)
TAPS = tuple(np.asarray(np.array(COEF) / SCALE, dtype=jnp.bfloat16).astype(np.float64).tolist())
STEPS = 4
NX, NY, NZ = 32, 32, 128
GROUP = 8 * NY
GROUPS = NX // 8
PAD = 4 * NY
CELLS = NX * NY


def difference_matrix(size, blocks):
    plus = np.zeros((size, size))
    for k in range(1, 5):
        plus += TAPS[k - 1] * (np.eye(size, k=k) - np.eye(size, k=1 - k))
    return np.kron(np.eye(blocks), plus)


def split(values):
    high = values.astype(jnp.bfloat16)
    low = (values - high.astype(jnp.float32)).astype(jnp.bfloat16)
    return jnp.concatenate([high, low], axis=1)


def along_y(matrix, parts):
    both = jnp.dot(matrix, parts, preferred_element_type=jnp.float32)
    return both[:, :NZ] + both[:, NZ:]


def along_z(parts, matrix):
    return jnp.dot(parts, matrix, preferred_element_type=jnp.float32)


def along_x(ref, base, backward):
    first = base + PAD - (NY if backward else 0)

    def plane(k):
        return ref[pl.ds(first + k * NY, GROUP), :]

    total = None
    for k in range(1, 5):
        term = TAPS[k - 1] * (plane(k) - plane(1 - k))
        total = term if total is None else total + term
    return total


def evolve_kernel(
    ap, src, wave, recs, resid, yplus_ref, yminus_ref, zplus_ref, zminus_ref,
    model, fwd, adj, image,
    pres, vel0, vel1, vel2, bulk, buoy, dpres, dvel, bulk_im, buoy_im,
):
    corner = ap[0, 0] // 4
    for j in range(16):
        slot = lax.rem(corner + j, 16)
        rows = pl.ds(j * 2 * NY, 2 * NY)
        bulk[rows, :] = SCALE * model[slot, 0]
        buoy[rows, :] = SCALE * model[slot, 1]
    edge = jnp.zeros((PAD, NZ), jnp.float32)
    for ref in (pres, vel0):
        ref[0:PAD, :] = edge
        ref[PAD + CELLS :, :] = edge
    lanes = lax.broadcasted_iota(jnp.int32, (1, NZ), 1)

    def load(state):
        for g in range(GROUPS):
            rows = pl.ds(g * GROUP, GROUP)
            padded = pl.ds(PAD + g * GROUP, GROUP)
            pres[padded, :] = state[0, 0, rows, :].astype(jnp.float32)
            vel0[padded, :] = state[0, 1, rows, :].astype(jnp.float32)
            vel1[rows, :] = state[0, 2, rows, :].astype(jnp.float32)
            vel2[rows, :] = state[0, 3, rows, :].astype(jnp.float32)

    def step(n, adjoint, first):
        for g in range(GROUPS):
            base = g * GROUP
            rows = pl.ds(base, GROUP)
            padded = pl.ds(PAD + base, GROUP)
            light = buoy[rows, :]
            parts = split(pres[padded, :])
            changes = (
                light * along_x(pres, base, False),
                light * along_y(yplus_ref[...], parts),
                light * along_z(parts, zplus_ref[...]),
            )
            total = None
            for d, (ref, where) in enumerate(((vel0, padded), (vel1, rows), (vel2, rows))):
                moved = ref[where, :] + changes[d]
                ref[where, :] = moved
                if adjoint:
                    term = dvel[n, d, rows, :] * moved
                    total = term if total is None else total + term
                else:
                    dvel[n, d, rows, :] = changes[d]
            if adjoint:
                buoy_im[rows, :] = total if first else buoy_im[rows, :] + total
        for g in range(GROUPS):
            base = g * GROUP
            rows = pl.ds(base, GROUP)
            padded = pl.ds(PAD + base, GROUP)
            divergence = (
                along_x(vel0, base, True)
                + along_y(yminus_ref[...], split(vel1[rows, :]))
                + along_z(split(vel2[rows, :]), zminus_ref[...])
            )
            change = bulk[rows, :] * divergence
            moved = pres[padded, :] + change
            pres[padded, :] = moved
            if adjoint:
                term = dpres[n, rows, :] * moved
                bulk_im[rows, :] = term if first else bulk_im[rows, :] + term
            else:
                dpres[n, rows, :] = change
        if adjoint:
            for j in range(NX):
                row = j * NY + recs[0, 2 * j]
                added = jnp.where(lanes == recs[0, 2 * j + 1], resid[0, n * NX + j], 0.0)
                at = pl.ds(row, 1)
                pres[pl.ds(PAD + row, 1), :] += added
                bulk_im[at, :] += dpres[n, at, :] * added
        else:
            row = src[0, 0] * NY + src[0, 1]
            added = jnp.where(lanes == src[0, 2], wave[0, n], 0.0)
            pres[pl.ds(PAD + row, 1), :] += added
            dpres[n, pl.ds(row, 1), :] += added

    load(fwd)

    def forward(n, carry):
        step(n, False, False)
        return carry

    lax.fori_loop(0, STEPS, forward, 0)
    load(adj)
    bulk_im[...] = jnp.zeros_like(bulk_im)
    buoy_im[...] = jnp.zeros_like(buoy_im)

    def backward(n, carry):
        step(STEPS - 1 - n, True, False)
        return carry

    lax.fori_loop(0, STEPS, backward, 0)
    for j in range(16):
        slot = lax.rem(corner + j, 16)
        rows = pl.ds(j * 2 * NY, 2 * NY)
        image[slot, 0] = bulk_im[rows, :]
        image[slot, 1] = buoy_im[rows, :]


def evolve(model, fwd_state, adj_state, aperture, src_pos, wavelet, rec_pos, residual):
    yplus = difference_matrix(NY, 8)
    zplus = difference_matrix(NZ, 1)
    matrices = [
        jnp.asarray(m, jnp.bfloat16)
        for m in (yplus, -yplus.T, np.concatenate([zplus.T, zplus.T]), np.concatenate([-zplus, -zplus]))
    ]
    smem = pl.BlockSpec(memory_space=pltpu.SMEM)
    vmem = pl.BlockSpec(memory_space=pltpu.VMEM)
    field = pltpu.VMEM((CELLS, NZ), jnp.float32)
    wide = pltpu.VMEM((CELLS + 2 * PAD, NZ), jnp.float32)
    return pl.pallas_call(
        evolve_kernel,
        out_shape=jax.ShapeDtypeStruct((16, 2, 2 * NY, NZ), jnp.float32),
        in_specs=[smem] * 5 + [vmem] * 7,
        out_specs=vmem,
        scratch_shapes=[
            wide, wide, field, field, field, field,
            pltpu.VMEM((STEPS, CELLS, NZ), jnp.float32),
            pltpu.VMEM((STEPS, 3, CELLS, NZ), jnp.float32),
            field, field,
        ],
        compiler_params=pltpu.CompilerParams(vmem_limit_bytes=40 * 1024 * 1024),
        cost_estimate=pl.CostEstimate(flops=10**9, bytes_accessed=5 * 2**20, transcendentals=0),
    )(
        aperture, src_pos, wavelet, rec_pos.reshape(1, -1), residual.reshape(1, -1), *matrices, model,
        fwd_state.reshape(1, 4, CELLS, NZ), adj_state.reshape(1, 4, CELLS, NZ),
    )

MESH = pl.DeviceIdType.MESH
FIELDS = 2
TILES = 4


def place():
    tile = lax.axis_index("tile")
    return tile // 8, lax.rem(tile // 2, 4), lax.rem(tile, 2)


def tile_at(x, y, core):
    return lax.rem(x + 4, 4) * 8 + lax.rem(y + 4, 4) * 2 + lax.rem(core, 2)


def remote(source, target, send, receive, device):
    return pltpu.make_async_remote_copy(
        src_ref=source, dst_ref=target, send_sem=send, recv_sem=receive,
        device_id=device, device_id_type=MESH,
    )


def greet(devices):
    barrier = pltpu.get_barrier_semaphore()
    for device in devices:
        pl.semaphore_signal(barrier, inc=1, device_id=device, device_id_type=MESH)
    return lambda: pl.semaphore_wait(barrier, len(devices))


def matches(code, residue):
    corner, level = code >> 2, code & 3
    upper = corner > residue
    return [
        [jnp.logical_and(level == t, upper if high else jnp.logical_not(upper)) for t in range(TILES)]
        for high in range(2)
    ]


def gather_kernel(
    ap, speed, density, model, codes, row, staged, x_send, x_recv, c_send, c_recv, y_send, y_recv
):
    x, y, core = place()
    right, left = {"tile": tile_at(x + 1, y, core)}, {"tile": tile_at(x - 1, y, core)}
    ahead = [{"tile": tile_at(x, y + j // 2, core + j % 2)} for j in range(8)]
    back = [{"tile": tile_at(x, y - j // 2, core + j % 2)} for j in range(8)]
    ready = greet([right, left] + ahead[1:])
    codes[0] = jnp.zeros((8, NZ), jnp.int32) + ap[0, 0]
    for t in range(TILES):
        dense, fast = density[t], speed[t]
        row[0, x, t] = dense * fast * fast
        row[1, x, t] = 1.0 / dense
    ready()
    xl, xr, x2 = lax.rem(x + 3, 4), lax.rem(x + 1, 4), lax.rem(x + 2, 4)
    pending = []

    def start(copy):
        copy.start()
        pending.append(copy)

    for j in range(1, 8):
        start(remote(codes.at[0], codes.at[j], c_send.at[j], c_recv.at[j], ahead[j]))
    for f in range(FIELDS):
        for side, device in ((0, right), (1, left)):
            start(remote(row.at[f, x], row.at[f, x], x_send.at[0, side, f], x_recv.at[0, side, f], device))

    def forward(f):
        for side, device, origin in ((0, right, xl), (1, left, xr)):
            part = row.at[f, origin]
            remote(part, part, x_send.at[0, side, f], x_recv.at[0, side, f], device).wait_recv()
            half = row.at[f, origin, pl.ds(2 * side, 2)]
            start(remote(half, half, x_send.at[1, side, f], x_recv.at[1, side, f], device))

    def passed_on(f):
        for side, device in ((0, right), (1, left)):
            half = row.at[f, x2, pl.ds(2 * side, 2)]
            remote(half, half, x_send.at[1, side, f], x_recv.at[1, side, f], device).wait_recv()

    def select(code, parity, f):
        found = matches(code, parity * 8 + y * 2 + core)
        chosen = jnp.zeros((8, 8, NZ), jnp.float32)
        for high in range(2):
            for t in range(TILES):
                chosen = jnp.where(found[high][t][None], row[f, parity + 2 * high, t], chosen)
        return chosen

    mine = y * 2 + core

    def serve(parity, own, f):
        for j in (2, 3, 6, 7, 4, 5, 1):
            if own == 0 and f == 0:
                remote(codes.at[0], codes.at[j], c_send.at[j], c_recv.at[j], ahead[j]).wait_recv()
            staged[own, f, j] = select(codes[j], parity, f)
            start(
                remote(
                    staged.at[own, f, j], model.at[parity, mine, f],
                    y_send.at[own, f, j], y_recv.at[own, f, j], back[j],
                )
            )
        model[parity, mine, f] = select(codes[0], parity, f)

    other, same = lax.rem(x + 1, 2), lax.rem(x, 2)
    forward(0)
    serve(other, 0, 0)
    forward(1)
    serve(other, 0, 1)
    passed_on(0)
    serve(same, 1, 0)
    passed_on(1)
    serve(same, 1, 1)
    for own, parity in ((0, other), (1, same)):
        for f in range(FIELDS):
            for j in range(1, 8):
                origin = lax.rem(y + j // 2, 4) * 2 + lax.rem(core + j % 2, 2)
                remote(
                    staged.at[own, f, j], model.at[parity, origin, f],
                    y_send.at[own, f, j], y_recv.at[own, f, j], back[j],
                ).wait_recv()
    for copy in pending:
        copy.wait_send()


def gather(aperture, speed, density):
    vmem = pl.BlockSpec(memory_space=pltpu.VMEM)
    dma = pltpu.SemaphoreType.DMA
    return pl.pallas_call(
        gather_kernel,
        out_shape=(
            jax.ShapeDtypeStruct((2, 8, FIELDS, 8, 8, NZ), jnp.float32),
            jax.ShapeDtypeStruct((8, 8, NZ), jnp.int32),
        ),
        in_specs=[pl.BlockSpec(memory_space=pltpu.SMEM), vmem, vmem],
        out_specs=(vmem, vmem),
        scratch_shapes=[
            pltpu.VMEM((FIELDS, 4, TILES, 8, 8, NZ), jnp.float32),
            pltpu.VMEM((2, FIELDS, 8, 8, 8, NZ), jnp.float32),
            dma((2, 2, FIELDS)), dma((2, 2, FIELDS)), dma((8,)), dma((8,)),
            dma((2, FIELDS, 8)), dma((2, FIELDS, 8)),
        ],
        compiler_params=pltpu.CompilerParams(
            collective_id=0, has_side_effects=True, vmem_limit_bytes=16 * 1024 * 1024
        ),
        cost_estimate=pl.CostEstimate(flops=10**6, bytes_accessed=60 * 2**20, transcendentals=0),
    )(aperture, speed.reshape(TILES, 8, 8, NZ), density.reshape(TILES, 8, 8, NZ))


def scatter_kernel(
    codes, image, speed, density, grad_speed, grad_density,
    came, part, passed, summed, total, terms,
    y_send, y_recv, x_send, x_recv, z_send, z_recv, g_send, g_recv,
):
    z = lax.axis_index("grp")
    x, y, core = place()
    right, left = {"tile": tile_at(x + 1, y, core)}, {"tile": tile_at(x - 1, y, core)}
    ahead = [{"tile": tile_at(x, y + j // 2, core + j % 2)} for j in range(8)]
    column = [{"grp": lax.rem(z + d, 8)} for d in range(8)]
    greet([right, left] + ahead[1:] + column[1:])()
    xl, xr, x2 = lax.rem(x + 3, 4), lax.rem(x + 1, 4), lax.rem(x + 2, 4)
    mine = y * 2 + core
    pending = []

    def start(copy):
        copy.start()
        pending.append(copy)

    other, same = lax.rem(x + 1, 2), lax.rem(x, 2)
    chunks = [(own, parity, f) for own, parity in ((1, same), (0, other)) for f in range(FIELDS)]

    def image_copy(own, parity, f, j):
        target = lax.rem(y + j // 2, 4) * 2 + lax.rem(core + j % 2, 2)
        return remote(
            image.at[parity, target, f], came.at[own, f, j], y_send.at[own, f, j], y_recv.at[own, f, j], ahead[j]
        )

    for own, parity, f in chunks:
        for j in (2, 3, 6, 7, 4, 5, 1):
            start(image_copy(own, parity, f, j))

    def collect(own, parity, f):
        for j in range(1, 8):
            image_copy(own, parity, f, j).wait_recv()
        found = [matches(codes[j], parity * 8 + mine) for j in range(8)]
        for high in range(2):
            for t in range(TILES):
                held = None
                for j in range(8):
                    values = image[parity, mine, f] if j == 0 else came[own, f, j]
                    term = jnp.where(found[j][high][t][None], values, 0.0)
                    held = term if held is None else held + term
                part[f, parity + 2 * high, t] = held

    def hop(stage, side, f):
        device, target = ((right, xr), (left, xl))[side]
        if stage == 0:
            return remote(
                part.at[f, x2, pl.ds(2 * side, 2)], passed.at[side, f],
                x_send.at[0, side, f], x_recv.at[0, side, f], device,
            )
        return remote(
            part.at[f, target], summed.at[side, f], x_send.at[1, side, f], x_recv.at[1, side, f], device
        )

    def piece_copy(f, d):
        return remote(
            total.at[f, lax.rem(z + d, 8)], terms.at[f, d], z_send.at[f, d], z_recv.at[f, d], column[d]
        )

    for f in range(FIELDS):
        collect(1, same, f)
        for side in range(2):
            start(hop(0, side, f))
    for f in range(FIELDS):
        collect(0, other, f)
        for side in range(2):
            target = (xr, xl)[side]
            hop(0, side, f).wait_recv()
            for i in range(2):
                part[f, target, 2 * side + i] += passed[side, f, i]
            start(hop(1, side, f))
    for f in range(FIELDS):
        for side in range(2):
            hop(1, side, f).wait_recv()
        for t in range(TILES):
            whole = part[f, x, t] + summed[0, f, t] + summed[1, f, t]
            total[f, 2 * t] = whole[:4]
            total[f, 2 * t + 1] = whole[4:]
        for d in (1, 7, 2, 6, 3, 5, 4):
            start(piece_copy(f, d))
    sums = []
    for f in range(FIELDS):
        whole = total[f, z]
        for d in range(1, 8):
            piece_copy(f, d).wait_recv()
            whole = whole + terms[f, d]
        sums.append(whole)
    fast, dense = speed[z], density[z]
    factor = 1.0 / math.sqrt(256.0)
    grad_speed[z] = factor * (sums[0] * (2.0 * dense * fast))
    grad_density[z] = factor * (sums[0] * (fast * fast) - sums[1] / (dense * dense))

    def result_copy(i, d, piece):
        ref = (grad_speed, grad_density)[i]
        return remote(ref.at[piece], ref.at[piece], g_send.at[i, d], g_recv.at[i, d], column[d])

    for d in (1, 7, 2, 6, 3, 5, 4):
        for i in range(2):
            start(result_copy(i, d, z))
    for d in range(1, 8):
        for i in range(2):
            result_copy(i, d, lax.rem(z + 8 - d, 8)).wait_recv()
    for copy in pending:
        copy.wait_send()


def scatter(codes, image, speed, density):
    vmem = pl.BlockSpec(memory_space=pltpu.VMEM)
    dma = pltpu.SemaphoreType.DMA
    shape = jax.ShapeDtypeStruct((8, 4, 8, NZ), jnp.float32)
    return pl.pallas_call(
        scatter_kernel,
        out_shape=(shape, shape),
        in_specs=[vmem] * 4,
        out_specs=(vmem, vmem),
        scratch_shapes=[
            pltpu.VMEM((2, FIELDS, 8, 8, 8, NZ), jnp.float32),
            pltpu.VMEM((FIELDS, 4, TILES, 8, 8, NZ), jnp.float32),
            pltpu.VMEM((2, FIELDS, 2, 8, 8, NZ), jnp.float32),
            pltpu.VMEM((2, FIELDS, TILES, 8, 8, NZ), jnp.float32),
            pltpu.VMEM((FIELDS, 8, 4, 8, NZ), jnp.float32),
            pltpu.VMEM((FIELDS, 8, 4, 8, NZ), jnp.float32),
            dma((2, FIELDS, 8)), dma((2, FIELDS, 8)), dma((2, 2, FIELDS)), dma((2, 2, FIELDS)),
            dma((FIELDS, 8)), dma((FIELDS, 8)), dma((2, 8)), dma((2, 8)),
        ],
        compiler_params=pltpu.CompilerParams(
            collective_id=1, has_side_effects=True, vmem_limit_bytes=16 * 1024 * 1024
        ),
        cost_estimate=pl.CostEstimate(flops=10**6, bytes_accessed=60 * 2**20, transcendentals=0),
    )(codes, image, speed.reshape(8, 4, 8, NZ), density.reshape(8, 4, 8, NZ))


def per_device(speed, density, fwd_state, adj_state, aperture, src_pos, wavelet, rec_pos, residual):
    model, codes = gather(aperture, speed, density)
    image = evolve(
        model.reshape(16, FIELDS, 2 * NY, NZ), fwd_state, adj_state, aperture, src_pos, wavelet, rec_pos, residual
    )
    grads = scatter(codes, image.reshape(2, 8, FIELDS, 8, 8, NZ), speed, density)
    return tuple(grad.reshape(speed.shape) for grad in grads)


def solution(mesh):
    return jax.shard_map(
        per_device,
        mesh=mesh,
        in_specs=(
            P("tile", None, None, None),
            P("tile", None, None, None),
            P(("grp", "tile"), None, None, None, None),
            P(("grp", "tile"), None, None, None, None),
            P(("grp", "tile"), None),
            P(("grp", "tile"), None),
            P(("grp", "tile"), None),
            P(("grp", "tile"), None, None),
            P(("grp", "tile"), None, None),
        ),
        out_specs=(P("tile", None, None, None), P("tile", None, None, None)),
        check_vma=False,
    )
```

```python
import math

import jax
import jax.numpy as jnp
import numpy as np
from jax import lax
from jax.experimental import pallas as pl
from jax.experimental.pallas import tpu as pltpu
from jax.sharding import PartitionSpec as P

COEF = (1225.0 / 1024.0, -245.0 / 3072.0, 49.0 / 5120.0, -5.0 / 7168.0)
SCALE = COEF[0] / (165.0 / 128.0)
TAPS = tuple(np.asarray(np.array(COEF) / SCALE, dtype=jnp.bfloat16).astype(np.float64).tolist())
STEPS = 4
NX, NY, NZ = 32, 32, 128
GROUP = 8 * NY
GROUPS = NX // 8
PAD = 4 * NY
CELLS = NX * NY


def difference_matrix(size, blocks):
    plus = np.zeros((size, size))
    for k in range(1, 5):
        plus += TAPS[k - 1] * (np.eye(size, k=k) - np.eye(size, k=1 - k))
    return np.kron(np.eye(blocks), plus)


def split(values):
    high = values.astype(jnp.bfloat16)
    low = (values - high.astype(jnp.float32)).astype(jnp.bfloat16)
    return jnp.concatenate([high, low], axis=1)


def along_y(matrix, parts):
    both = jnp.dot(matrix, parts, preferred_element_type=jnp.float32)
    return both[:, :NZ] + both[:, NZ:]


def along_z(parts, matrix):
    return jnp.dot(parts, matrix, preferred_element_type=jnp.float32)


def along_x(ref, base, backward):
    def plane(k):
        return ref[pl.ds(base + PAD + (k - backward) * NY, GROUP), :]

    total = None
    for k in range(1, 5):
        term = TAPS[k - 1] * (plane(k) - plane(1 - k))
        total = term if total is None else total + term
    return total


MESH = pl.DeviceIdType.MESH
FIELDS = 2
TILES = 4


def place():
    tile = lax.axis_index("tile")
    return tile // 8, lax.rem(tile // 2, 4), lax.rem(tile, 2)


def tile_at(x, y, core):
    return lax.rem(x + 4, 4) * 8 + lax.rem(y + 4, 4) * 2 + lax.rem(core, 2)


def remote(source, target, send, receive, device):
    return pltpu.make_async_remote_copy(
        src_ref=source, dst_ref=target, send_sem=send, recv_sem=receive,
        device_id=device, device_id_type=MESH,
    )


def greet(devices):
    barrier = pltpu.get_barrier_semaphore()
    for device in devices:
        pl.semaphore_signal(barrier, inc=1, device_id=device, device_id_type=MESH)
    return lambda: pl.semaphore_wait(barrier, len(devices))


def matches(code, residue):
    corner, level = code >> 2, code & 3
    upper = corner > residue
    return [
        [jnp.logical_and(level == t, upper if high else jnp.logical_not(upper)) for t in range(TILES)]
        for high in range(2)
    ]


ORDER = (2, 3, 6, 7, 4, 5, 1)


def kernel(
    ap, src, wave, recs, resid, speed_in, density_in, fwd_in, adj_in, yplus_in, yminus_in, zplus_in, zminus_in,
    grad_speed, grad_density,
    speed, density, fwd, adj, yplus, yminus, zplus, zminus, in_sems,
    row, staged, bulk_tiles, buoy_tiles, codes, x_send, x_recv, c_send, c_recv, y_send, y_recv,
    pres, vel0, vel1, vel2, apres, avel0, avel1, avel2, bulk, buoy, dpres, dvel, bulk_image, buoy_image,
    image, came, part, passed, summed, total, terms,
    iy_send, iy_recv, ix_send, ix_recv, z_send, z_recv, g_send, g_recv,
):
    z = lax.axis_index("grp")
    x, y, core = place()
    right, left = {"tile": tile_at(x + 1, y, core)}, {"tile": tile_at(x - 1, y, core)}
    ahead = [{"tile": tile_at(x, y + j // 2, core + j % 2)} for j in range(8)]
    back = [{"tile": tile_at(x, y - j // 2, core + j % 2)} for j in range(8)]
    column = [{"grp": lax.rem(z + d, 8)} for d in range(8)]
    ready = greet([right, left] + ahead[1:] + column[1:])
    loads = [
        pltpu.make_async_copy(source, target, in_sems.at[i])
        for i, (source, target) in enumerate(
            (
                (density_in, density), (speed_in, speed), (fwd_in, fwd), (adj_in, adj),
                (yplus_in, yplus), (zplus_in, zplus), (yminus_in, yminus), (zminus_in, zminus),
            )
        )
    ]
    for load in loads:
        load.start()
    codes[0] = jnp.zeros((8, NZ), jnp.int32) + ap[0, 0]
    loads[0].wait()
    loads[1].wait()
    for t in range(TILES):
        dense = density[t]
        row[1, x, t] = 1.0 / dense
    for t in range(TILES):
        dense, fast = density[t], speed[t]
        row[0, x, t] = dense * fast * fast
    models, images = (bulk_tiles, buoy_tiles), (bulk_image, buoy_image)
    xl, xr, x2 = lax.rem(x + 3, 4), lax.rem(x + 1, 4), lax.rem(x + 2, 4)
    other, same = lax.rem(x + 1, 2), lax.rem(x, 2)
    mine = y * 2 + core
    pending = []

    def start(copy):
        copy.start()
        pending.append(copy)

    ready()
    for f in (1, 0):
        for side, device in ((0, right), (1, left)):
            start(remote(row.at[f, x], row.at[f, x], x_send.at[0, side, f], x_recv.at[0, side, f], device))
        if f == 1:
            for j in range(1, 8):
                start(remote(codes.at[0], codes.at[j], c_send.at[j], c_recv.at[j], ahead[j]))

    edge = jnp.zeros((PAD, NZ), jnp.float32)
    for ref in (pres, vel0, apres, avel0):
        ref[0:PAD, :] = edge
        ref[PAD + CELLS :, :] = edge
    forward_refs = (pres, vel0, vel1, vel2)
    adjoint_refs = (apres, avel0, avel1, avel2)

    def rows_of(g):
        return pl.ds(g * GROUP, GROUP)

    def padded_of(g):
        return pl.ds(PAD + g * GROUP, GROUP)

    def spots(g):
        return (padded_of(g), padded_of(g), rows_of(g), rows_of(g))

    def unpack(state, refs):
        for g in range(GROUPS):
            for i, (ref, spot) in enumerate(zip(refs, spots(g))):
                ref[spot, :] = state[0, i, rows_of(g), :].astype(jnp.float32)

    def differences(ref, g):
        parts = split(ref[padded_of(g), :])
        return (
            along_x(ref, g * GROUP, 0),
            along_y(yplus[...], parts),
            along_z(parts, zplus[...]),
        )

    def divergence(refs, g):
        return (
            along_x(refs[1], g * GROUP, 1)
            + along_y(yminus[...], split(refs[2][rows_of(g), :]))
            + along_z(split(refs[3][rows_of(g), :]), zminus[...])
        )

    cell = lax.broadcasted_iota(jnp.int32, (NY, NZ), 0) * NZ + lax.broadcasted_iota(jnp.int32, (NY, NZ), 1)
    fired = (src[0, 0] * NY + src[0, 1]) * NZ + src[0, 2]

    def source(n, g):
        planes = []
        for i in range(8):
            planes.append(jnp.where(cell == fired - (g * 8 + i) * NY * NZ, wave[0, n], 0.0))
        return jnp.concatenate(planes, axis=0)

    def received(n, g):
        planes = []
        for i in range(8):
            j = g * 8 + i
            planes.append(jnp.where(cell == recs[0, 0, j] * NZ + recs[0, 1, j], resid[0, n, j], 0.0))
        return jnp.concatenate(planes, axis=0)

    for load in loads[2:]:
        load.wait()
    for state, refs, slot in ((fwd, forward_refs, 0), (adj, adjoint_refs, 1)):
        unpack(state, refs)
        for g in range(GROUPS):
            for d, values in enumerate(differences(refs[0], g)):
                dvel[slot, d, rows_of(g), :] = values

    def forward(f):
        for side, device, origin in ((0, right, xl), (1, left, xr)):
            whole = row.at[f, origin]
            remote(whole, whole, x_send.at[0, side, f], x_recv.at[0, side, f], device).wait_recv()
            half = row.at[f, origin, pl.ds(2 * side, 2)]
            start(remote(half, half, x_send.at[1, side, f], x_recv.at[1, side, f], device))

    def passed_on(f):
        for side, device in ((0, right), (1, left)):
            half = row.at[f, x2, pl.ds(2 * side, 2)]
            remote(half, half, x_send.at[1, side, f], x_recv.at[1, side, f], device).wait_recv()

    def select(code, parity, f):
        found = matches(code, parity * 8 + mine)
        chosen = jnp.zeros((8, 8, NZ), jnp.float32)
        for high in range(2):
            for t in range(TILES):
                chosen = jnp.where(found[high][t][None], row[f, parity + 2 * high, t], chosen)
        return chosen

    def serve(parity, own, f):
        for j in ORDER:
            if own == 0 and f == 1:
                remote(codes.at[0], codes.at[j], c_send.at[j], c_recv.at[j], ahead[j]).wait_recv()
            staged[own, f, j] = select(codes[j], parity, f)
            start(
                remote(
                    staged.at[own, f, j], models[f].at[parity * 8 + mine],
                    y_send.at[own, f, j], y_recv.at[own, f, j], back[j],
                )
            )
        models[f][parity * 8 + mine] = select(codes[0], parity, f)

    def arrived(f):
        for own, parity in ((0, other), (1, same)):
            for j in range(1, 8):
                origin = lax.rem(y + j // 2, 4) * 2 + lax.rem(core + j % 2, 2)
                remote(
                    staged.at[own, f, j], models[f].at[parity * 8 + origin],
                    y_send.at[own, f, j], y_recv.at[own, f, j], back[j],
                ).wait_recv()

    forward(1)
    serve(other, 0, 1)
    passed_on(1)
    serve(same, 1, 1)
    forward(0)
    serve(other, 0, 0)
    passed_on(0)
    serve(same, 1, 0)

    corner = ap[0, 0] >> 2

    def place_model(f, ref):
        for j in range(16):
            values = models[f][(corner + j) & 15]
            ref[pl.ds(j * 2 * NY, 2 * NY), :] = SCALE * values.reshape(2 * NY, NZ)

    arrived(1)
    place_model(1, buoy)
    for g in range(GROUPS):
        light = buoy[rows_of(g), :]
        for d in range(3):
            spot = spots(g)[1 + d]
            change = light * dvel[0, d, rows_of(g), :]
            dvel[0, d, rows_of(g), :] = change
            forward_refs[1 + d][spot, :] += change
            adjoint_refs[1 + d][spot, :] += light * dvel[1, d, rows_of(g), :]
    for g in range(GROUPS):
        dpres[0, rows_of(g), :] = divergence(forward_refs, g)
        dpres[1, rows_of(g), :] = divergence(adjoint_refs, g)
    arrived(0)
    place_model(0, bulk)
    for g in range(GROUPS):
        stiff = bulk[rows_of(g), :]
        change = stiff * dpres[0, rows_of(g), :] + source(0, g)
        dpres[0, rows_of(g), :] = change
        pres[padded_of(g), :] += change
        apres[padded_of(g), :] += stiff * dpres[1, rows_of(g), :] + received(STEPS - 1, g)

    def move(refs, g):
        light = buoy[rows_of(g), :]
        changes, moved = [], []
        for d, values in enumerate(differences(refs[0], g)):
            change = light * values
            after = refs[1 + d][spots(g)[1 + d], :] + change
            refs[1 + d][spots(g)[1 + d], :] = after
            changes.append(change)
            moved.append(after)
        return changes, moved

    def set_image(f, g, values):
        images[f][4 * g : 4 * g + 4] = values.reshape(4, 2 * NY, NZ)

    def get_image(f, g):
        return images[f][4 * g : 4 * g + 4].reshape(GROUP, NZ)

    def inner(changes, others):
        return changes[0] * others[0] + changes[1] * others[1] + changes[2] * others[2]

    def replay(n, carry):
        for g in range(GROUPS):
            changes, _ = move(forward_refs, g)
            for d in range(3):
                dvel[n, d, rows_of(g), :] = changes[d]
        for g in range(GROUPS):
            change = bulk[rows_of(g), :] * divergence(forward_refs, g) + source(n, g)
            dpres[n, rows_of(g), :] = change
            pres[padded_of(g), :] += change
        return carry

    lax.fori_loop(1, STEPS - 1, replay, 0)
    for g in range(GROUPS):
        changes, _ = move(forward_refs, g)
        set_image(1, g, inner(changes, [adjoint_refs[1 + d][spots(g)[1 + d], :] for d in range(3)]))
    for g in range(GROUPS):
        change = bulk[rows_of(g), :] * divergence(forward_refs, g) + source(STEPS - 1, g)
        set_image(0, g, change * apres[padded_of(g), :])

    def adjoint_velocities(n):
        for g in range(GROUPS):
            _, moved = move(adjoint_refs, g)
            set_image(1, g, get_image(1, g) + inner([dvel[n, d, rows_of(g), :] for d in range(3)], moved))

    def adjoint_pressure(n):
        for g in range(GROUPS):
            after = (
                apres[padded_of(g), :]
                + bulk[rows_of(g), :] * divergence(adjoint_refs, g)
                + received(n, g)
            )
            apres[padded_of(g), :] = after
            set_image(0, g, get_image(0, g) + dpres[n, rows_of(g), :] * after)

    def back_step(i, carry):
        adjoint_velocities(STEPS - 2 - i)
        adjoint_pressure(STEPS - 2 - i)
        return carry

    lax.fori_loop(0, STEPS - 2, back_step, 0)

    def image_copy(own, parity, f, j):
        target = lax.rem(y + j // 2, 4) * 2 + lax.rem(core + j % 2, 2)
        return remote(
            image.at[f, parity * 8 + target], came.at[own, f, j], iy_send.at[own, f, j], iy_recv.at[own, f, j], ahead[j]
        )

    def send_image(f):
        for r in range(16):
            image[f, r] = images[f][(r + 16 - corner) & 15].reshape(8, 8, NZ)
        for own, parity in ((1, same), (0, other)):
            for j in ORDER:
                start(image_copy(own, parity, f, j))

    def collect(own, parity, f):
        for j in range(1, 8):
            image_copy(own, parity, f, j).wait_recv()
        found = [matches(codes[j], parity * 8 + mine) for j in range(8)]
        for high in range(2):
            for t in range(TILES):
                held = None
                for j in range(8):
                    values = image[f, parity * 8 + mine] if j == 0 else came[own, f, j]
                    term = jnp.where(found[j][high][t][None], values, 0.0)
                    held = term if held is None else held + term
                part[f, parity + 2 * high, t] = held

    def hop(stage, side, f):
        device, target = ((right, xr), (left, xl))[side]
        if stage == 0:
            return remote(
                part.at[f, x2, pl.ds(2 * side, 2)], passed.at[side, f],
                ix_send.at[0, side, f], ix_recv.at[0, side, f], device,
            )
        return remote(
            part.at[f, target], summed.at[side, f], ix_send.at[1, side, f], ix_recv.at[1, side, f], device
        )

    def piece_copy(f, d):
        return remote(
            total.at[f, lax.rem(z + d, 8)], terms.at[f, d], z_send.at[f, d], z_recv.at[f, d], column[d]
        )

    def send_on(f):
        for side in range(2):
            target = (xr, xl)[side]
            hop(0, side, f).wait_recv()
            for i in range(2):
                part[f, target, 2 * side + i] += passed[side, f, i]
            start(hop(1, side, f))

    def send_pieces(f):
        for side in range(2):
            hop(1, side, f).wait_recv()
        for t in range(TILES):
            whole = part[f, x, t] + summed[0, f, t] + summed[1, f, t]
            total[f, 2 * t] = whole[:4]
            total[f, 2 * t + 1] = whole[4:]
        for d in (4, 3, 5, 2, 6, 1, 7):
            start(piece_copy(f, d))

    def collect_same(f):
        collect(1, same, f)
        for side in range(2):
            start(hop(0, side, f))

    def collect_other(f):
        collect(0, other, f)
        send_on(f)

    adjoint_velocities(0)
    send_image(1)
    adjoint_pressure(0)
    send_image(0)
    collect_same(1)
    collect_other(1)
    collect_same(0)
    send_pieces(1)
    collect_other(0)
    send_pieces(0)
    sums = []
    for f in range(FIELDS):
        whole = total[f, z]
        for d in range(1, 8):
            piece_copy(f, d).wait_recv()
            whole = whole + terms[f, d]
        sums.append(whole)
    half = pl.ds(4 * lax.rem(z, 2), 4)
    fast, dense = speed[z // 2, half], density[z // 2, half]
    factor = 1.0 / math.sqrt(256.0)
    grad_speed[z] = factor * (sums[0] * (2.0 * dense * fast))
    grad_density[z] = factor * (sums[0] * (fast * fast) - sums[1] / (dense * dense))

    def result_copy(i, d, piece):
        ref = (grad_speed, grad_density)[i]
        return remote(ref.at[piece], ref.at[piece], g_send.at[i, d], g_recv.at[i, d], column[d])

    for d in (4, 3, 5, 2, 6, 1, 7):
        for i in range(2):
            start(result_copy(i, d, z))
    for d in range(1, 8):
        for i in range(2):
            result_copy(i, d, lax.rem(z + 8 - d, 8)).wait_recv()
    for copy in pending:
        copy.wait_send()


def per_device(speed, density, fwd_state, adj_state, aperture, src_pos, wavelet, rec_pos, residual):
    yplus = difference_matrix(NY, 8)
    zplus = difference_matrix(NZ, 1)
    matrices = [
        jnp.asarray(m, jnp.bfloat16)
        for m in (yplus, -yplus.T, np.concatenate([zplus.T, zplus.T]), np.concatenate([-zplus, -zplus]))
    ]
    smem = pl.BlockSpec(memory_space=pltpu.SMEM)
    vmem = pl.BlockSpec(memory_space=pltpu.VMEM)
    whole = pl.BlockSpec(memory_space=pl.ANY)
    dma = pltpu.SemaphoreType.DMA

    def floats(*shape):
        return pltpu.VMEM(shape + (NZ,), jnp.float32)

    def halves(*shape):
        return pltpu.VMEM(shape, jnp.bfloat16)

    tiles = floats(TILES, 8, 8)
    field, wide = floats(CELLS), floats(CELLS + 2 * PAD)
    shape = jax.ShapeDtypeStruct((8, 4, 8, NZ), jnp.float32)
    grads = pl.pallas_call(
        kernel,
        out_shape=(shape, shape),
        in_specs=[smem] * 5 + [whole] * 8,
        out_specs=(vmem, vmem),
        scratch_shapes=[
            tiles, tiles, halves(1, 4, CELLS, NZ), halves(1, 4, CELLS, NZ),
            halves(GROUP, GROUP), halves(GROUP, GROUP), halves(2 * NZ, NZ), halves(2 * NZ, NZ), dma((8,)),
            floats(FIELDS, 4, TILES, 8, 8), floats(2, FIELDS, 8, 8, 8), floats(16, 8, 8), floats(16, 8, 8),
            pltpu.VMEM((8, 8, NZ), jnp.int32),
            dma((2, 2, FIELDS)), dma((2, 2, FIELDS)), dma((8,)), dma((8,)), dma((2, FIELDS, 8)), dma((2, FIELDS, 8)),
            wide, wide, field, field, wide, wide, field, field, field, field,
            floats(STEPS - 1, CELLS), floats(STEPS - 1, 3, CELLS), floats(16, 2 * NY), floats(16, 2 * NY),
            floats(FIELDS, 16, 8, 8), floats(2, FIELDS, 8, 8, 8), floats(FIELDS, 4, TILES, 8, 8),
            floats(2, FIELDS, 2, 8, 8), floats(2, FIELDS, TILES, 8, 8),
            floats(FIELDS, 8, 4, 8), floats(FIELDS, 8, 4, 8),
            dma((2, FIELDS, 8)), dma((2, FIELDS, 8)), dma((2, 2, FIELDS)), dma((2, 2, FIELDS)),
            dma((FIELDS, 8)), dma((FIELDS, 8)), dma((2, 8)), dma((2, 8)),
        ],
        compiler_params=pltpu.CompilerParams(
            collective_id=0, has_side_effects=True, vmem_limit_bytes=56 * 1024 * 1024
        ),
    )(
        aperture, src_pos, wavelet, rec_pos.transpose(0, 2, 1), residual,
        speed.reshape(TILES, 8, 8, NZ), density.reshape(TILES, 8, 8, NZ),
        fwd_state.reshape(1, 4, CELLS, NZ), adj_state.reshape(1, 4, CELLS, NZ), *matrices,
    )
    return tuple(grad.reshape(speed.shape) for grad in grads)


def solution(mesh):
    return jax.shard_map(
        per_device,
        mesh=mesh,
        in_specs=(
            P("tile", None, None, None),
            P("tile", None, None, None),
            P(("grp", "tile"), None, None, None, None),
            P(("grp", "tile"), None, None, None, None),
            P(("grp", "tile"), None),
            P(("grp", "tile"), None),
            P(("grp", "tile"), None),
            P(("grp", "tile"), None, None),
            P(("grp", "tile"), None, None),
        ),
        out_specs=(P("tile", None, None, None), P("tile", None, None, None)),
        check_vma=False,
    )
```

```python
import math

import jax
import jax.numpy as jnp
import numpy as np
from jax import lax
from jax.experimental import pallas as pl
from jax.experimental.pallas import tpu as pltpu
from jax.sharding import PartitionSpec as P

COEF = (1225.0 / 1024.0, -245.0 / 3072.0, 49.0 / 5120.0, -5.0 / 7168.0)
SCALE = COEF[0] / (165.0 / 128.0)
TAPS = tuple(np.asarray(np.array(COEF) / SCALE, dtype=jnp.bfloat16).astype(np.float64).tolist())
STEPS = 4
NX, NY, NZ = 32, 32, 128
GROUP = 8 * NY
GROUPS = NX // 8
PAD = 4 * NY
CELLS = NX * NY


def difference_matrix(size, blocks):
    plus = np.zeros((size, size))
    for k in range(1, 5):
        plus += TAPS[k - 1] * (np.eye(size, k=k) - np.eye(size, k=1 - k))
    return np.kron(np.eye(blocks), plus)


def split(values):
    high = values.astype(jnp.bfloat16)
    low = (values - high.astype(jnp.float32)).astype(jnp.bfloat16)
    return jnp.concatenate([high, low], axis=1)


def along_y(matrix, parts):
    both = jnp.dot(matrix, parts, preferred_element_type=jnp.float32)
    return both[:, :NZ] + both[:, NZ:]


def along_z(parts, matrix):
    return jnp.dot(parts, matrix, preferred_element_type=jnp.float32)


def along_x(ref, base, backward):
    def plane(k):
        return ref[pl.ds(base + PAD + (k - backward) * NY, GROUP), :]

    total = None
    for k in range(1, 5):
        term = TAPS[k - 1] * (plane(k) - plane(1 - k))
        total = term if total is None else total + term
    return total


MESH = pl.DeviceIdType.MESH
FIELDS = 2
HALVES = 2
TILES = 4


def place():
    tile = lax.axis_index("tile")
    return tile // 8, lax.rem(tile // 2, 4), lax.rem(tile, 2)


def tile_at(x, y, core):
    return lax.rem(x + 4, 4) * 8 + lax.rem(y + 4, 4) * 2 + lax.rem(core, 2)


def remote(source, target, send, receive, device):
    return pltpu.make_async_remote_copy(
        src_ref=source, dst_ref=target, send_sem=send, recv_sem=receive,
        device_id=device, device_id_type=MESH,
    )


def greet(devices):
    barrier = pltpu.get_barrier_semaphore()
    for device in devices:
        pl.semaphore_signal(barrier, inc=1, device_id=device, device_id_type=MESH)
    return lambda: pl.semaphore_wait(barrier, len(devices))


def matches(code, residue):
    corner, level = code >> 2, code & 3
    upper = corner > residue
    return [
        [jnp.logical_and(level == t, upper if high else jnp.logical_not(upper)) for t in range(TILES)]
        for high in range(2)
    ]


ORDER = (4, 5, 2, 3, 6, 7, 1)
FAR = (4, 3, 5, 2, 6, 1, 7)


def kernel(
    ap, src, wave, recs, resid, speed_in, density_in, fwd_in, adj_in, yplus_in, yminus_in, zplus_in, zminus_in,
    grad_speed, grad_density,
    speed, density, fwd, adj, yplus, yminus, zplus, zminus, in_sems,
    row, staged, bulk_tiles, buoy_tiles, codes, x_send, x_recv, c_send, c_recv, y_send, y_recv,
    pres, vel0, vel1, vel2, apres, avel0, avel1, avel2, bulk, buoy, dpres, dvel, bulk_image, buoy_image,
    image, came, part, passed, summed, total, terms, sums,
    iy_send, iy_recv, ix_send, ix_recv, z_send, z_recv, g_send, g_recv,
):
    z = lax.axis_index("grp")
    x, y, core = place()
    right, left = {"tile": tile_at(x + 1, y, core)}, {"tile": tile_at(x - 1, y, core)}
    ahead = [{"tile": tile_at(x, y + j // 2, core + j % 2)} for j in range(8)]
    back = [{"tile": tile_at(x, y - j // 2, core + j % 2)} for j in range(8)]
    column = [{"grp": lax.rem(z + d, 8)} for d in range(8)]
    ready = greet([right, left] + ahead[1:] + column[1:])
    loads = [
        pltpu.make_async_copy(source, target, in_sems.at[i])
        for i, (source, target) in enumerate(
            (
                (density_in, density), (speed_in, speed), (fwd_in, fwd), (adj_in, adj),
                (yplus_in, yplus), (zplus_in, zplus), (yminus_in, yminus), (zminus_in, zminus),
            )
        )
    ]
    for load in loads:
        load.start()
    codes[0] = jnp.zeros((8, NZ), jnp.int32) + ap[0, 0]
    loads[0].wait()
    loads[1].wait()
    for t in range(TILES):
        dense = density[t]
        row[1, x, t] = 1.0 / dense
    for t in range(TILES):
        dense, fast = density[t], speed[t]
        row[0, x, t] = dense * fast * fast
    models, images = (bulk_tiles, buoy_tiles), (bulk_image, buoy_image)
    xl, xr, x2 = lax.rem(x + 3, 4), lax.rem(x + 1, 4), lax.rem(x + 2, 4)
    other, same = lax.rem(x + 1, 2), lax.rem(x, 2)
    mine = y * 2 + core
    pending = []

    def start(copy):
        copy.start()
        pending.append(copy)

    def row_copy(f, side, origin):
        part = row.at[f, origin]
        return remote(part, part, x_send.at[0, side, f], x_recv.at[0, side, f], (right, left)[side])

    def half_copy(f, side, origin):
        part = row.at[f, origin, pl.ds(2 * side, 2)]
        return remote(part, part, x_send.at[1, side, f], x_recv.at[1, side, f], (right, left)[side])

    ready()
    for f in (1, 0):
        for side in range(2):
            start(row_copy(f, side, x))
        if f == 1:
            for j in range(1, 8):
                start(remote(codes.at[0], codes.at[j], c_send.at[j], c_recv.at[j], ahead[j]))

    edge = jnp.zeros((PAD, NZ), jnp.float32)
    for ref in (pres, vel0, apres, avel0):
        ref[0:PAD, :] = edge
        ref[PAD + CELLS :, :] = edge
    forward_refs = (pres, vel0, vel1, vel2)
    adjoint_refs = (apres, avel0, avel1, avel2)

    def rows_of(g):
        return pl.ds(g * GROUP, GROUP)

    def padded_of(g):
        return pl.ds(PAD + g * GROUP, GROUP)

    def spots(g):
        return (padded_of(g), padded_of(g), rows_of(g), rows_of(g))

    def unpack(state, refs):
        for g in range(GROUPS):
            for i, (ref, spot) in enumerate(zip(refs, spots(g))):
                ref[spot, :] = state[0, i, rows_of(g), :].astype(jnp.float32)

    def differences(ref, g):
        parts = split(ref[padded_of(g), :])
        return (
            along_x(ref, g * GROUP, 0),
            along_y(yplus[...], parts),
            along_z(parts, zplus[...]),
        )

    def divergence(refs, g):
        return (
            along_x(refs[1], g * GROUP, 1)
            + along_y(yminus[...], split(refs[2][rows_of(g), :]))
            + along_z(split(refs[3][rows_of(g), :]), zminus[...])
        )

    cell = lax.broadcasted_iota(jnp.int32, (NY, NZ), 0) * NZ + lax.broadcasted_iota(jnp.int32, (NY, NZ), 1)
    fired = (src[0, 0] * NY + src[0, 1]) * NZ + src[0, 2]

    def source(n, g):
        planes = []
        for i in range(8):
            planes.append(jnp.where(cell == fired - (g * 8 + i) * NY * NZ, wave[0, n], 0.0))
        return jnp.concatenate(planes, axis=0)

    def received(n, g):
        planes = []
        for i in range(8):
            j = g * 8 + i
            planes.append(jnp.where(cell == recs[0, 0, j] * NZ + recs[0, 1, j], resid[0, n, j], 0.0))
        return jnp.concatenate(planes, axis=0)

    for load in loads[2:]:
        load.wait()
    for state, refs, slot in ((fwd, forward_refs, 0), (adj, adjoint_refs, 1)):
        unpack(state, refs)
        for g in range(GROUPS):
            for d, values in enumerate(differences(refs[0], g)):
                dvel[slot, d, rows_of(g), :] = values

    def select(code, parity, f):
        found = matches(code, parity * 8 + mine)
        chosen = jnp.zeros((8, 8, NZ), jnp.float32)
        for high in range(2):
            for t in range(TILES):
                chosen = jnp.where(found[high][t][None], row[f, parity + 2 * high, t], chosen)
        return chosen

    def tile_copy(parity, own, f, j, origin):
        return remote(
            staged.at[own, f, j], models[f].at[parity * 8 + origin], y_send.at[own, f, j], y_recv.at[own, f, j], back[j]
        )

    def serve(parity, own, f):
        for j in ORDER:
            if own == 0 and f == 1:
                remote(codes.at[0], codes.at[j], c_send.at[j], c_recv.at[j], ahead[j]).wait_recv()
            staged[own, f, j] = select(codes[j], parity, f)
            start(tile_copy(parity, own, f, j, mine))
        models[f][parity * 8 + mine] = select(codes[0], parity, f)

    def arrived(f):
        for own, parity in ((0, other), (1, same)):
            for j in range(1, 8):
                origin = lax.rem(y + j // 2, 4) * 2 + lax.rem(core + j % 2, 2)
                tile_copy(parity, own, f, j, origin).wait_recv()

    for f in (1, 0):
        for side, origin in ((0, xl), (1, xr)):
            row_copy(f, side, origin).wait_recv()
            start(half_copy(f, side, origin))
        serve(other, 0, f)
    for f in (1, 0):
        for side in range(2):
            half_copy(f, side, x2).wait_recv()
        serve(same, 1, f)

    corner = ap[0, 0] >> 2

    def place_model(f, ref):
        for j in range(16):
            values = models[f][(corner + j) & 15]
            ref[pl.ds(j * 2 * NY, 2 * NY), :] = SCALE * values.reshape(2 * NY, NZ)

    arrived(1)
    place_model(1, buoy)
    for g in range(GROUPS):
        light = buoy[rows_of(g), :]
        for d in range(3):
            spot = spots(g)[1 + d]
            change = light * dvel[0, d, rows_of(g), :]
            dvel[0, d, rows_of(g), :] = change
            forward_refs[1 + d][spot, :] += change
            adjoint_refs[1 + d][spot, :] += light * dvel[1, d, rows_of(g), :]
    for g in range(GROUPS):
        dpres[0, rows_of(g), :] = divergence(forward_refs, g)
        dpres[1, rows_of(g), :] = divergence(adjoint_refs, g)
    arrived(0)
    place_model(0, bulk)
    for g in range(GROUPS):
        stiff = bulk[rows_of(g), :]
        change = stiff * dpres[0, rows_of(g), :] + source(0, g)
        dpres[0, rows_of(g), :] = change
        pres[padded_of(g), :] += change
        apres[padded_of(g), :] += stiff * dpres[1, rows_of(g), :] + received(STEPS - 1, g)

    def move(refs, g):
        light = buoy[rows_of(g), :]
        changes, moved = [], []
        for d, values in enumerate(differences(refs[0], g)):
            change = light * values
            after = refs[1 + d][spots(g)[1 + d], :] + change
            refs[1 + d][spots(g)[1 + d], :] = after
            changes.append(change)
            moved.append(after)
        return changes, moved

    def set_image(f, g, values):
        images[f][4 * g : 4 * g + 4] = values.reshape(4, 2 * NY, NZ)

    def get_image(f, g):
        return images[f][4 * g : 4 * g + 4].reshape(GROUP, NZ)

    def inner(changes, others):
        return changes[0] * others[0] + changes[1] * others[1] + changes[2] * others[2]

    def replay(n, carry):
        for g in range(GROUPS):
            changes, _ = move(forward_refs, g)
            for d in range(3):
                dvel[n, d, rows_of(g), :] = changes[d]
        for g in range(GROUPS):
            change = bulk[rows_of(g), :] * divergence(forward_refs, g) + source(n, g)
            dpres[n, rows_of(g), :] = change
            pres[padded_of(g), :] += change
        return carry

    lax.fori_loop(1, STEPS - 1, replay, 0)
    for g in range(GROUPS):
        changes, _ = move(forward_refs, g)
        set_image(1, g, inner(changes, [adjoint_refs[1 + d][spots(g)[1 + d], :] for d in range(3)]))
    for g in range(GROUPS):
        change = bulk[rows_of(g), :] * divergence(forward_refs, g) + source(STEPS - 1, g)
        set_image(0, g, change * apres[padded_of(g), :])

    def adjoint_velocities(n):
        for g in range(GROUPS):
            _, moved = move(adjoint_refs, g)
            set_image(1, g, get_image(1, g) + inner([dvel[n, d, rows_of(g), :] for d in range(3)], moved))

    def adjoint_pressure(n):
        for g in range(GROUPS):
            after = (
                apres[padded_of(g), :]
                + bulk[rows_of(g), :] * divergence(adjoint_refs, g)
                + received(n, g)
            )
            apres[padded_of(g), :] = after
            set_image(0, g, get_image(0, g) + dpres[n, rows_of(g), :] * after)

    def back_step(i, carry):
        adjoint_velocities(STEPS - 2 - i)
        adjoint_pressure(STEPS - 2 - i)
        return carry

    lax.fori_loop(0, STEPS - 2, back_step, 0)

    def image_copy(own, parity, f, j):
        target = lax.rem(y + j // 2, 4) * 2 + lax.rem(core + j % 2, 2)
        return remote(
            image.at[f, parity * 8 + target], came.at[own, f, j], iy_send.at[own, f, j], iy_recv.at[own, f, j], ahead[j]
        )

    def send_image(f):
        for r in range(16):
            image[f, r] = images[f][(r + 16 - corner) & 15].reshape(8, 8, NZ)
        for own, parity in ((1, same), (0, other)):
            for j in ORDER:
                start(image_copy(own, parity, f, j))

    def collect(own, parity, f, h):
        if h == 0:
            for j in range(1, 8):
                image_copy(own, parity, f, j).wait_recv()
        found = [matches(codes[j], parity * 8 + mine) for j in range(8)]
        rows = pl.ds(4 * h, 4)
        for high in range(2):
            for t in range(TILES):
                held = None
                for j in range(8):
                    values = image[f, parity * 8 + mine, rows] if j == 0 else came[own, f, j, rows]
                    term = jnp.where(found[j][high][t][None], values, 0.0)
                    held = term if held is None else held + term
                part[f, h, parity + 2 * high, t] = held

    def hop(stage, side, f, h):
        device, target = ((right, xr), (left, xl))[side]
        if stage == 0:
            origin, landing = part.at[f, h, x2, pl.ds(2 * side, 2)], passed.at[side, f, h]
        else:
            origin, landing = part.at[f, h, target], summed.at[side, f, h]
        return remote(origin, landing, ix_send.at[stage, side, f, h], ix_recv.at[stage, side, f, h], device)

    def collect_same(f):
        for h in range(HALVES):
            collect(1, same, f, h)
            for side in range(2):
                start(hop(0, side, f, h))

    def collect_other(f):
        for h in range(HALVES):
            collect(0, other, f, h)
            for side, target in ((0, xr), (1, xl)):
                hop(0, side, f, h).wait_recv()
                for i in range(2):
                    part[f, h, target, 2 * side + i] += passed[side, f, h, i]
                start(hop(1, side, f, h))

    def piece_copy(f, h, d):
        return remote(
            total.at[f, h, lax.rem(z + d, 8)], terms.at[f, h, d], z_send.at[f, h, d], z_recv.at[f, h, d], column[d]
        )

    def result_copy(f, h, d, piece):
        part_sum = sums.at[f, h, piece]
        return remote(part_sum, part_sum, g_send.at[f, h, d], g_recv.at[f, h, d], column[d])

    def send_pieces(f):
        for h in range(HALVES):
            for side in range(2):
                hop(1, side, f, h).wait_recv()
            for t in range(TILES):
                whole = part[f, h, x, t] + summed[0, f, h, t] + summed[1, f, h, t]
                total[f, h, 2 * t] = whole[:2]
                total[f, h, 2 * t + 1] = whole[2:]
            for d in FAR:
                start(piece_copy(f, h, d))

    def finish_pieces(f):
        for h in range(HALVES):
            held = total[f, h, z]
            for d in range(1, 8):
                piece_copy(f, h, d).wait_recv()
                held = held + terms[f, h, d]
            sums[f, h, z] = held
            for d in FAR:
                start(result_copy(f, h, d, z))

    adjoint_velocities(0)
    send_image(1)
    adjoint_pressure(0)
    send_image(0)
    collect_same(1)
    collect_other(1)
    collect_same(0)
    send_pieces(1)
    collect_other(0)
    send_pieces(0)
    finish_pieces(1)
    finish_pieces(0)
    for f in (1, 0):
        for h in range(HALVES):
            for d in range(1, 8):
                result_copy(f, h, d, lax.rem(z + 8 - d, 8)).wait_recv()
    for h in range(HALVES):
        for piece in range(8):
            t, spot = piece // 2, pl.ds(4 * h + 2 * (piece % 2), 2)
            fast, dense = speed[t, spot], density[t, spot]
            stiff, light = sums[0, h, piece], sums[1, h, piece]
            grad_speed[t, spot] = stiff * (2.0 * dense * fast)
            grad_density[t, spot] = stiff * (fast * fast) - light / (dense * dense)
    for copy in pending:
        copy.wait_send()


def per_device(speed, density, fwd_state, adj_state, aperture, src_pos, wavelet, rec_pos, residual):
    yplus = difference_matrix(NY, 8)
    zplus = difference_matrix(NZ, 1)
    matrices = [
        jnp.asarray(m, jnp.bfloat16)
        for m in (yplus, -yplus.T, np.concatenate([zplus.T, zplus.T]), np.concatenate([-zplus, -zplus]))
    ]
    smem = pl.BlockSpec(memory_space=pltpu.SMEM)
    vmem = pl.BlockSpec(memory_space=pltpu.VMEM)
    whole = pl.BlockSpec(memory_space=pl.ANY)
    dma = pltpu.SemaphoreType.DMA

    def floats(*shape):
        return pltpu.VMEM(shape + (NZ,), jnp.float32)

    def halves(*shape):
        return pltpu.VMEM(shape, jnp.bfloat16)

    tiles = floats(TILES, 8, 8)
    field, wide = floats(CELLS), floats(CELLS + 2 * PAD)
    shape = jax.ShapeDtypeStruct((TILES, 8, 8, NZ), jnp.float32)
    grads = pl.pallas_call(
        kernel,
        out_shape=(shape, shape),
        in_specs=[smem] * 5 + [whole] * 8,
        out_specs=(vmem, vmem),
        scratch_shapes=[
            tiles, tiles, halves(1, 4, CELLS, NZ), halves(1, 4, CELLS, NZ),
            halves(GROUP, GROUP), halves(GROUP, GROUP), halves(2 * NZ, NZ), halves(2 * NZ, NZ), dma((8,)),
            floats(FIELDS, 4, TILES, 8, 8), floats(2, FIELDS, 8, 8, 8), floats(16, 8, 8), floats(16, 8, 8),
            pltpu.VMEM((8, 8, NZ), jnp.int32),
            dma((2, 2, FIELDS)), dma((2, 2, FIELDS)), dma((8,)), dma((8,)), dma((2, FIELDS, 8)), dma((2, FIELDS, 8)),
            wide, wide, field, field, wide, wide, field, field, field, field,
            floats(STEPS - 1, CELLS), floats(STEPS - 1, 3, CELLS), floats(16, 2 * NY), floats(16, 2 * NY),
            floats(FIELDS, 16, 8, 8), floats(2, FIELDS, 8, 8, 8), floats(FIELDS, HALVES, 4, TILES, 4, 8),
            floats(2, FIELDS, HALVES, 2, 4, 8), floats(2, FIELDS, HALVES, TILES, 4, 8),
            floats(FIELDS, HALVES, 8, 2, 8), floats(FIELDS, HALVES, 8, 2, 8), floats(FIELDS, HALVES, 8, 2, 8),
            dma((2, FIELDS, 8)), dma((2, FIELDS, 8)),
            dma((2, 2, FIELDS, HALVES)), dma((2, 2, FIELDS, HALVES)),
            dma((FIELDS, HALVES, 8)), dma((FIELDS, HALVES, 8)), dma((FIELDS, HALVES, 8)), dma((FIELDS, HALVES, 8)),
        ],
        compiler_params=pltpu.CompilerParams(
            collective_id=0, has_side_effects=True, vmem_limit_bytes=56 * 1024 * 1024
        ),
    )(
        aperture, src_pos, wavelet, rec_pos.transpose(0, 2, 1), residual,
        speed.reshape(TILES, 8, 8, NZ), density.reshape(TILES, 8, 8, NZ),
        fwd_state.reshape(1, 4, CELLS, NZ), adj_state.reshape(1, 4, CELLS, NZ), *matrices,
    )
    factor = 1.0 / math.sqrt(lax.axis_size("grp") * lax.axis_size("tile"))
    return tuple(factor * grad.reshape(speed.shape) for grad in grads)


def solution(mesh):
    return jax.shard_map(
        per_device,
        mesh=mesh,
        in_specs=(
            P("tile", None, None, None),
            P("tile", None, None, None),
            P(("grp", "tile"), None, None, None, None),
            P(("grp", "tile"), None, None, None, None),
            P(("grp", "tile"), None),
            P(("grp", "tile"), None),
            P(("grp", "tile"), None),
            P(("grp", "tile"), None, None),
            P(("grp", "tile"), None, None),
        ),
        out_specs=(P("tile", None, None, None), P("tile", None, None, None)),
        check_vma=False,
    )
```

```python
import math

import jax
import jax.numpy as jnp
import numpy as np
from jax import lax
from jax.experimental import pallas as pl
from jax.experimental.pallas import tpu as pltpu
from jax.sharding import PartitionSpec as P

COEF = (1225.0 / 1024.0, -245.0 / 3072.0, 49.0 / 5120.0, -5.0 / 7168.0)
SCALE = COEF[0] / (165.0 / 128.0)
TAPS = tuple(np.asarray(np.array(COEF) / SCALE, dtype=jnp.bfloat16).astype(np.float64).tolist())
STEPS = 4
NX, NY, NZ = 32, 32, 128
GROUP = 8 * NY
GROUPS = NX // 8
PAD = 4 * NY
CELLS = NX * NY


def difference_matrix(size, blocks):
    plus = np.zeros((size, size))
    for k in range(1, 5):
        plus += TAPS[k - 1] * (np.eye(size, k=k) - np.eye(size, k=1 - k))
    return np.kron(np.eye(blocks), plus)


def split(values):
    high = values.astype(jnp.bfloat16)
    low = (values - high.astype(jnp.float32)).astype(jnp.bfloat16)
    return jnp.concatenate([high, low], axis=1)


def along_y(matrix, parts):
    both = jnp.dot(matrix, parts, preferred_element_type=jnp.float32)
    return both[:, :NZ] + both[:, NZ:]


def along_z(parts, matrix):
    return jnp.dot(parts, matrix, preferred_element_type=jnp.float32)


def along_x(ref, base, backward):
    def plane(k):
        return ref[pl.ds(base + PAD + (k - backward) * NY, GROUP), :]

    total = None
    for k in range(1, 5):
        term = TAPS[k - 1] * (plane(k) - plane(1 - k))
        total = term if total is None else total + term
    return total


MESH = pl.DeviceIdType.MESH
FIELDS = 2
HALVES = 2
TILES = 4


def place():
    tile = lax.axis_index("tile")
    return tile // 8, lax.rem(tile // 2, 4), lax.rem(tile, 2)


def tile_at(x, y, core):
    return lax.rem(x + 4, 4) * 8 + lax.rem(y + 4, 4) * 2 + lax.rem(core, 2)


def remote(source, target, send, receive, device):
    return pltpu.make_async_remote_copy(
        src_ref=source, dst_ref=target, send_sem=send, recv_sem=receive,
        device_id=device, device_id_type=MESH,
    )


def greet(devices):
    barrier = pltpu.get_barrier_semaphore()
    for device in devices:
        pl.semaphore_signal(barrier, inc=1, device_id=device, device_id_type=MESH)
    return lambda: pl.semaphore_wait(barrier, len(devices))


def matches(code, residue):
    corner, level = code >> 2, code & 3
    upper = corner > residue
    return [
        [jnp.logical_and(level == t, upper if high else jnp.logical_not(upper)) for t in range(TILES)]
        for high in range(2)
    ]


ORDER = (4, 5, 2, 3, 6, 7, 1)
FAR = (4, 3, 5, 2, 6, 1, 7)


def kernel(
    ap, src, wave, recs, resid, speed_in, density_in, fwd_in, adj_in, yplus_in, yminus_in, zplus_in, zminus_in,
    bulk_sum, buoy_sum,
    speed, density, fwd, adj, yplus, yminus, zplus, zminus, in_sems,
    row, staged, bulk_tiles, buoy_tiles, codes, x_send, x_recv, c_send, c_recv, y_send, y_recv,
    pres, vel0, vel1, vel2, apres, avel0, avel1, avel2, bulk, buoy, dpres, dvel, bulk_image, buoy_image,
    image, came, part, passed, summed, total, terms, sums,
    iy_send, iy_recv, ix_send, ix_recv, z_send, z_recv, g_send, g_recv, keep_sems,
):
    z = lax.axis_index("grp")
    x, y, core = place()
    right, left = {"tile": tile_at(x + 1, y, core)}, {"tile": tile_at(x - 1, y, core)}
    ahead = [{"tile": tile_at(x, y + j // 2, core + j % 2)} for j in range(8)]
    back = [{"tile": tile_at(x, y - j // 2, core + j % 2)} for j in range(8)]
    column = [{"grp": lax.rem(z + d, 8)} for d in range(8)]
    ready = greet([right, left] + ahead[1:] + column[1:])
    loads = [
        pltpu.make_async_copy(source, target, in_sems.at[i])
        for i, (source, target) in enumerate(
            (
                (density_in, density), (speed_in, speed), (fwd_in, fwd), (adj_in, adj),
                (yplus_in, yplus), (zplus_in, zplus), (yminus_in, yminus), (zminus_in, zminus),
            )
        )
    ]
    for load in loads[:2]:
        load.start()
    codes[0] = jnp.zeros((8, NZ), jnp.int32) + ap[0, 0]
    loads[0].wait()
    for t in range(TILES):
        row[1, x, t] = 1.0 / density[t]
    for load in loads[2:]:
        load.start()
    models, images = (bulk_tiles, buoy_tiles), (bulk_image, buoy_image)
    xl, xr, x2 = lax.rem(x + 3, 4), lax.rem(x + 1, 4), lax.rem(x + 2, 4)
    other, same = lax.rem(x + 1, 2), lax.rem(x, 2)
    mine = y * 2 + core
    pending = []

    def start(copy):
        copy.start()
        pending.append(copy)

    def row_copy(f, side, origin):
        part = row.at[f, origin]
        return remote(part, part, x_send.at[0, side, f], x_recv.at[0, side, f], (right, left)[side])

    def half_copy(f, side, origin):
        part = row.at[f, origin, pl.ds(2 * side, 2)]
        return remote(part, part, x_send.at[1, side, f], x_recv.at[1, side, f], (right, left)[side])

    ready()
    for side in range(2):
        start(row_copy(1, side, x))
    for j in range(1, 8):
        start(remote(codes.at[0], codes.at[j], c_send.at[j], c_recv.at[j], ahead[j]))
    loads[1].wait()
    for t in range(TILES):
        fast = speed[t]
        row[0, x, t] = density[t] * fast * fast
    for side in range(2):
        start(row_copy(0, side, x))

    edge = jnp.zeros((PAD, NZ), jnp.float32)
    for ref in (pres, vel0, apres, avel0):
        ref[0:PAD, :] = edge
        ref[PAD + CELLS :, :] = edge
    forward_refs = (pres, vel0, vel1, vel2)
    adjoint_refs = (apres, avel0, avel1, avel2)

    def rows_of(g):
        return pl.ds(g * GROUP, GROUP)

    def padded_of(g):
        return pl.ds(PAD + g * GROUP, GROUP)

    def spots(g):
        return (padded_of(g), padded_of(g), rows_of(g), rows_of(g))

    def unpack(state, refs):
        for g in range(GROUPS):
            for i, (ref, spot) in enumerate(zip(refs, spots(g))):
                ref[spot, :] = state[0, i, rows_of(g), :].astype(jnp.float32)

    def differences(ref, g):
        parts = split(ref[padded_of(g), :])
        return (
            along_x(ref, g * GROUP, 0),
            along_y(yplus[...], parts),
            along_z(parts, zplus[...]),
        )

    def divergence(refs, g):
        return (
            along_x(refs[1], g * GROUP, 1)
            + along_y(yminus[...], split(refs[2][rows_of(g), :]))
            + along_z(split(refs[3][rows_of(g), :]), zminus[...])
        )

    cell = lax.broadcasted_iota(jnp.int32, (NY, NZ), 0) * NZ + lax.broadcasted_iota(jnp.int32, (NY, NZ), 1)
    fired = (src[0, 0] * NY + src[0, 1]) * NZ + src[0, 2]

    def source(n, g):
        planes = []
        for i in range(8):
            planes.append(jnp.where(cell == fired - (g * 8 + i) * NY * NZ, wave[0, n], 0.0))
        return jnp.concatenate(planes, axis=0)

    def received(n, g):
        planes = []
        for i in range(8):
            j = g * 8 + i
            planes.append(jnp.where(cell == recs[0, 0, j] * NZ + recs[0, 1, j], resid[0, n, j], 0.0))
        return jnp.concatenate(planes, axis=0)

    for load in loads[2:]:
        load.wait()
    for state, refs, slot in ((fwd, forward_refs, 0), (adj, adjoint_refs, 1)):
        unpack(state, refs)
        for g in range(GROUPS):
            for d, values in enumerate(differences(refs[0], g)):
                dvel[slot, d, rows_of(g), :] = values

    def select(code, parity, f):
        found = matches(code, parity * 8 + mine)
        chosen = jnp.zeros((8, 8, NZ), jnp.float32)
        for high in range(2):
            for t in range(TILES):
                chosen = jnp.where(found[high][t][None], row[f, parity + 2 * high, t], chosen)
        return chosen

    def tile_copy(parity, own, f, j, origin):
        return remote(
            staged.at[own, f, j], models[f].at[parity * 8 + origin], y_send.at[own, f, j], y_recv.at[own, f, j], back[j]
        )

    def serve(parity, own, f):
        for j in ORDER:
            if own == 0 and f == 1:
                remote(codes.at[0], codes.at[j], c_send.at[j], c_recv.at[j], ahead[j]).wait_recv()
            staged[own, f, j] = select(codes[j], parity, f)
            start(tile_copy(parity, own, f, j, mine))
        models[f][parity * 8 + mine] = select(codes[0], parity, f)

    def arrived(f):
        for own, parity in ((0, other), (1, same)):
            for j in range(1, 8):
                origin = lax.rem(y + j // 2, 4) * 2 + lax.rem(core + j % 2, 2)
                tile_copy(parity, own, f, j, origin).wait_recv()

    for f in (1, 0):
        for side, origin in ((0, xl), (1, xr)):
            row_copy(f, side, origin).wait_recv()
            start(half_copy(f, side, origin))
        serve(other, 0, f)
    for f in (1, 0):
        for side in range(2):
            half_copy(f, side, x2).wait_recv()
        serve(same, 1, f)

    corner = ap[0, 0] >> 2

    def place_model(f, ref):
        for j in range(16):
            values = models[f][(corner + j) & 15]
            ref[pl.ds(j * 2 * NY, 2 * NY), :] = SCALE * values.reshape(2 * NY, NZ)

    arrived(1)
    place_model(1, buoy)
    for g in range(GROUPS):
        light = buoy[rows_of(g), :]
        for d in range(3):
            spot = spots(g)[1 + d]
            change = light * dvel[0, d, rows_of(g), :]
            dvel[0, d, rows_of(g), :] = change
            forward_refs[1 + d][spot, :] += change
            adjoint_refs[1 + d][spot, :] += light * dvel[1, d, rows_of(g), :]
    for g in range(GROUPS):
        dpres[0, rows_of(g), :] = divergence(forward_refs, g)
        dpres[1, rows_of(g), :] = divergence(adjoint_refs, g)
    arrived(0)
    place_model(0, bulk)
    for g in range(GROUPS):
        stiff = bulk[rows_of(g), :]
        change = stiff * dpres[0, rows_of(g), :] + source(0, g)
        dpres[0, rows_of(g), :] = change
        pres[padded_of(g), :] += change
        apres[padded_of(g), :] += stiff * dpres[1, rows_of(g), :] + received(STEPS - 1, g)

    def move(refs, g):
        light = buoy[rows_of(g), :]
        changes, moved = [], []
        for d, values in enumerate(differences(refs[0], g)):
            change = light * values
            after = refs[1 + d][spots(g)[1 + d], :] + change
            refs[1 + d][spots(g)[1 + d], :] = after
            changes.append(change)
            moved.append(after)
        return changes, moved

    def set_image(f, g, values):
        images[f][4 * g : 4 * g + 4] = values.reshape(4, 2 * NY, NZ)

    def get_image(f, g):
        return images[f][4 * g : 4 * g + 4].reshape(GROUP, NZ)

    def inner(changes, others):
        return changes[0] * others[0] + changes[1] * others[1] + changes[2] * others[2]

    def replay(n, carry):
        for g in range(GROUPS):
            changes, _ = move(forward_refs, g)
            for d in range(3):
                dvel[n, d, rows_of(g), :] = changes[d]
        for g in range(GROUPS):
            change = bulk[rows_of(g), :] * divergence(forward_refs, g) + source(n, g)
            dpres[n, rows_of(g), :] = change
            pres[padded_of(g), :] += change
        return carry

    lax.fori_loop(1, STEPS - 1, replay, 0)
    for g in range(GROUPS):
        changes, _ = move(forward_refs, g)
        set_image(1, g, inner(changes, [adjoint_refs[1 + d][spots(g)[1 + d], :] for d in range(3)]))
    for g in range(GROUPS):
        change = bulk[rows_of(g), :] * divergence(forward_refs, g) + source(STEPS - 1, g)
        set_image(0, g, change * apres[padded_of(g), :])

    def adjoint_velocities(n):
        for g in range(GROUPS):
            _, moved = move(adjoint_refs, g)
            set_image(1, g, get_image(1, g) + inner([dvel[n, d, rows_of(g), :] for d in range(3)], moved))

    def adjoint_pressure(n):
        for g in range(GROUPS):
            after = (
                apres[padded_of(g), :]
                + bulk[rows_of(g), :] * divergence(adjoint_refs, g)
                + received(n, g)
            )
            apres[padded_of(g), :] = after
            set_image(0, g, get_image(0, g) + dpres[n, rows_of(g), :] * after)

    def back_step(i, carry):
        adjoint_velocities(STEPS - 2 - i)
        adjoint_pressure(STEPS - 2 - i)
        return carry

    lax.fori_loop(0, STEPS - 2, back_step, 0)

    def image_copy(own, parity, f, h, j):
        target = lax.rem(y + j // 2, 4) * 2 + lax.rem(core + j % 2, 2)
        rows = pl.ds(4 * h, 4)
        return remote(
            image.at[f, parity * 8 + target, rows], came.at[own, f, j, rows],
            iy_send.at[own, f, h, j], iy_recv.at[own, f, h, j], ahead[j],
        )

    def send_image(f):
        for r in range(16):
            image[f, r] = images[f][(r + 16 - corner) & 15].reshape(8, 8, NZ)
        for own, parity in ((1, same), (0, other)):
            for h in range(HALVES):
                for j in ORDER:
                    start(image_copy(own, parity, f, h, j))

    def collect(own, parity, f, h):
        for j in range(1, 8):
            image_copy(own, parity, f, h, j).wait_recv()
        found = [matches(codes[j], parity * 8 + mine) for j in range(8)]
        rows = pl.ds(4 * h, 4)
        for high in range(2):
            for t in range(TILES):
                held = None
                for j in range(8):
                    values = image[f, parity * 8 + mine, rows] if j == 0 else came[own, f, j, rows]
                    term = jnp.where(found[j][high][t][None], values, 0.0)
                    held = term if held is None else held + term
                part[f, h, parity + 2 * high, t] = held

    def hop(stage, side, f, h):
        device, target = ((right, xr), (left, xl))[side]
        if stage == 0:
            origin, landing = part.at[f, h, x2, pl.ds(2 * side, 2)], passed.at[side, f, h]
        else:
            origin, landing = part.at[f, h, target], summed.at[side, f, h]
        return remote(origin, landing, ix_send.at[stage, side, f, h], ix_recv.at[stage, side, f, h], device)

    def collect_same(f, h):
        collect(1, same, f, h)
        for side in range(2):
            start(hop(0, side, f, h))

    def collect_other(f, h):
        collect(0, other, f, h)
        for side, target in ((0, xr), (1, xl)):
            hop(0, side, f, h).wait_recv()
            for i in range(2):
                part[f, h, target, 2 * side + i] += passed[side, f, h, i]
            start(hop(1, side, f, h))

    def piece_copy(f, h, d):
        return remote(
            total.at[f, h, lax.rem(z + d, 8)], terms.at[f, h, d], z_send.at[f, h, d], z_recv.at[f, h, d], column[d]
        )

    outputs = (bulk_sum, buoy_sum)

    def place_of(f, h, piece):
        return outputs[f].at[piece // 2, pl.ds(4 * h + 2 * lax.rem(piece, 2), 2)]

    def result_copy(f, h, d, piece):
        return remote(sums.at[f, h], place_of(f, h, piece), g_send.at[f, h, d], g_recv.at[f, h, d], column[d])

    def keep_copy(f, h):
        return pltpu.make_async_copy(sums.at[f, h], place_of(f, h, z), keep_sems.at[f, h])

    def send_pieces(f, h):
        for side in range(2):
            hop(1, side, f, h).wait_recv()
        for t in range(TILES):
            whole = part[f, h, x, t] + summed[0, f, h, t] + summed[1, f, h, t]
            total[f, h, 2 * t] = whole[:2]
            total[f, h, 2 * t + 1] = whole[2:]
        for d in FAR:
            start(piece_copy(f, h, d))

    def finish_pieces(f, h):
        held = total[f, h, z]
        for d in range(1, 8):
            piece_copy(f, h, d).wait_recv()
            held = held + terms[f, h, d]
        sums[f, h] = held
        keep_copy(f, h).start()
        for d in FAR:
            start(result_copy(f, h, d, z))

    adjoint_velocities(0)
    send_image(1)
    adjoint_pressure(0)
    send_image(0)
    for h in range(HALVES):
        collect_same(1, h)
    for h in range(HALVES):
        collect_other(1, h)
    for h in range(HALVES):
        collect_same(0, h)
        send_pieces(1, h)
    for h in range(HALVES):
        collect_other(0, h)
    for h in range(HALVES):
        send_pieces(0, h)
    for f in (1, 0):
        for h in range(HALVES):
            finish_pieces(f, h)
    for f in (1, 0):
        for h in range(HALVES):
            for d in range(1, 8):
                result_copy(f, h, d, lax.rem(z + 8 - d, 8)).wait_recv()
    for f in range(FIELDS):
        for h in range(HALVES):
            keep_copy(f, h).wait()
    for copy in pending:
        copy.wait_send()


def per_device(speed, density, fwd_state, adj_state, aperture, src_pos, wavelet, rec_pos, residual):
    yplus = difference_matrix(NY, 8)
    zplus = difference_matrix(NZ, 1)
    matrices = [
        jnp.asarray(m, jnp.bfloat16)
        for m in (yplus, -yplus.T, np.concatenate([zplus.T, zplus.T]), np.concatenate([-zplus, -zplus]))
    ]
    smem = pl.BlockSpec(memory_space=pltpu.SMEM)
    whole = pl.BlockSpec(memory_space=pl.ANY)
    dma = pltpu.SemaphoreType.DMA

    def floats(*shape):
        return pltpu.VMEM(shape + (NZ,), jnp.float32)

    def halves(*shape):
        return pltpu.VMEM(shape, jnp.bfloat16)

    tiles = floats(TILES, 8, 8)
    field, wide = floats(CELLS), floats(CELLS + 2 * PAD)
    shape = jax.ShapeDtypeStruct((TILES, 8, 8, NZ), jnp.float32)
    sums = pl.pallas_call(
        kernel,
        out_shape=(shape, shape),
        in_specs=[smem] * 5 + [whole] * 8,
        out_specs=(whole, whole),
        scratch_shapes=[
            tiles, tiles, halves(1, 4, CELLS, NZ), halves(1, 4, CELLS, NZ),
            halves(GROUP, GROUP), halves(GROUP, GROUP), halves(2 * NZ, NZ), halves(2 * NZ, NZ), dma((8,)),
            floats(FIELDS, 4, TILES, 8, 8), floats(2, FIELDS, 8, 8, 8), floats(16, 8, 8), floats(16, 8, 8),
            pltpu.VMEM((8, 8, NZ), jnp.int32),
            dma((2, 2, FIELDS)), dma((2, 2, FIELDS)), dma((8,)), dma((8,)), dma((2, FIELDS, 8)), dma((2, FIELDS, 8)),
            wide, wide, field, field, wide, wide, field, field, field, field,
            floats(STEPS - 1, CELLS), floats(STEPS - 1, 3, CELLS), floats(16, 2 * NY), floats(16, 2 * NY),
            floats(FIELDS, 16, 8, 8), floats(2, FIELDS, 8, 8, 8), floats(FIELDS, HALVES, 4, TILES, 4, 8),
            floats(2, FIELDS, HALVES, 2, 4, 8), floats(2, FIELDS, HALVES, TILES, 4, 8),
            floats(FIELDS, HALVES, 8, 2, 8), floats(FIELDS, HALVES, 8, 2, 8), floats(FIELDS, HALVES, 2, 8),
            dma((2, FIELDS, HALVES, 8)), dma((2, FIELDS, HALVES, 8)),
            dma((2, 2, FIELDS, HALVES)), dma((2, 2, FIELDS, HALVES)),
            dma((FIELDS, HALVES, 8)), dma((FIELDS, HALVES, 8)), dma((FIELDS, HALVES, 8)), dma((FIELDS, HALVES, 8)),
            dma((FIELDS, HALVES)),
        ],
        compiler_params=pltpu.CompilerParams(
            collective_id=0, has_side_effects=True, vmem_limit_bytes=56 * 1024 * 1024
        ),
    )(
        aperture, src_pos, wavelet, rec_pos.transpose(0, 2, 1), residual,
        speed.reshape(TILES, 8, 8, NZ), density.reshape(TILES, 8, 8, NZ),
        fwd_state.reshape(1, 4, CELLS, NZ), adj_state.reshape(1, 4, CELLS, NZ), *matrices,
    )
    bulk_sum, buoy_sum = (values.reshape(speed.shape) for values in sums)
    factor = 1.0 / math.sqrt(lax.axis_size("grp") * lax.axis_size("tile"))
    grad_speed = factor * (bulk_sum * (2.0 * density * speed))
    grad_density = factor * (bulk_sum * (speed * speed) - buoy_sum / (density * density))
    return grad_speed, grad_density


def solution(mesh):
    return jax.shard_map(
        per_device,
        mesh=mesh,
        in_specs=(
            P("tile", None, None, None),
            P("tile", None, None, None),
            P(("grp", "tile"), None, None, None, None),
            P(("grp", "tile"), None, None, None, None),
            P(("grp", "tile"), None),
            P(("grp", "tile"), None),
            P(("grp", "tile"), None),
            P(("grp", "tile"), None, None),
            P(("grp", "tile"), None, None),
        ),
        out_specs=(P("tile", None, None, None), P("tile", None, None, None)),
        check_vma=False,
    )
```

```python
import math

import jax
import jax.numpy as jnp
import numpy as np
from jax import lax
from jax.experimental import pallas as pl
from jax.experimental.pallas import tpu as pltpu
from jax.sharding import PartitionSpec as P

COEF = (1225.0 / 1024.0, -245.0 / 3072.0, 49.0 / 5120.0, -5.0 / 7168.0)
SCALE = COEF[0] / (165.0 / 128.0)
TAPS = tuple(np.asarray(np.array(COEF) / SCALE, dtype=jnp.bfloat16).astype(np.float64).tolist())
STEPS = 4
NX, NY, NZ = 32, 32, 128
GROUP = 8 * NY
GROUPS = NX // 8
PAD = 4 * NY
CELLS = NX * NY


def difference_matrix(size, blocks):
    plus = np.zeros((size, size))
    for k in range(1, 5):
        plus += TAPS[k - 1] * (np.eye(size, k=k) - np.eye(size, k=1 - k))
    return np.kron(np.eye(blocks), plus)


def split(values):
    high = values.astype(jnp.bfloat16)
    low = (values - high.astype(jnp.float32)).astype(jnp.bfloat16)
    return jnp.concatenate([high, low], axis=1)


def along_y(matrix, parts):
    both = jnp.dot(matrix, parts, preferred_element_type=jnp.float32)
    return both[:, :NZ] + both[:, NZ:]


def along_z(parts, matrix):
    return jnp.dot(parts, matrix, preferred_element_type=jnp.float32)


def along_x(ref, base, backward):
    def plane(k):
        return ref[pl.ds(base + PAD + (k - backward) * NY, GROUP), :]

    total = None
    for k in range(1, 5):
        term = TAPS[k - 1] * (plane(k) - plane(1 - k))
        total = term if total is None else total + term
    return total


MESH = pl.DeviceIdType.MESH
FIELDS = 2
HALVES = 2
TILES = 4


def place():
    tile = lax.axis_index("tile")
    return tile // 8, lax.rem(tile // 2, 4), lax.rem(tile, 2)


def tile_at(x, y, core):
    return lax.rem(x + 4, 4) * 8 + lax.rem(y + 4, 4) * 2 + lax.rem(core, 2)


def remote(source, target, send, receive, device):
    return pltpu.make_async_remote_copy(
        src_ref=source, dst_ref=target, send_sem=send, recv_sem=receive,
        device_id=device, device_id_type=MESH,
    )


def greet(devices):
    barrier = pltpu.get_barrier_semaphore()
    for device in devices:
        pl.semaphore_signal(barrier, inc=1, device_id=device, device_id_type=MESH)
    return lambda: pl.semaphore_wait(barrier, len(devices))


def matches(code, residue):
    corner, level = code >> 2, code & 3
    upper = corner > residue
    return [
        [jnp.logical_and(level == t, upper if high else jnp.logical_not(upper)) for t in range(TILES)]
        for high in range(2)
    ]


ORDER = (2, 6, 4, 3, 7, 5, 1)
FAR = (4, 3, 5, 2, 6, 1, 7)


def kernel(
    ap, src, wave, recs, resid, speed_in, density_in, fwd_in, adj_in, yplus_in, yminus_in, zplus_in, zminus_in,
    bulk_sum, buoy_sum,
    speed, density, fwd, adj, yplus, yminus, zplus, zminus, in_sems,
    row, staged, bulk_tiles, buoy_tiles, codes, x_send, x_recv, c_send, c_recv, y_send, y_recv,
    pres, vel0, vel1, vel2, apres, avel0, avel1, avel2, bulk, buoy, dpres, dvel, bulk_image, buoy_image,
    image, came, part, passed, summed, total, terms, sums,
    iy_send, iy_recv, ix_send, ix_recv, z_send, z_recv, g_send, g_recv, keep_sems,
):
    z = lax.axis_index("grp")
    x, y, core = place()
    right, left = {"tile": tile_at(x + 1, y, core)}, {"tile": tile_at(x - 1, y, core)}
    ahead = [{"tile": tile_at(x, y + j // 2, core + j % 2)} for j in range(8)]
    back = [{"tile": tile_at(x, y - j // 2, core + j % 2)} for j in range(8)]
    column = [{"grp": lax.rem(z + d, 8)} for d in range(8)]
    ready = greet([right, left] + ahead[1:] + column[1:])
    loads = [
        pltpu.make_async_copy(source, target, in_sems.at[i])
        for i, (source, target) in enumerate(
            (
                (density_in, density), (speed_in, speed), (fwd_in, fwd), (adj_in, adj),
                (yplus_in, yplus), (zplus_in, zplus), (yminus_in, yminus), (zminus_in, zminus),
            )
        )
    ]
    for load in loads[:2]:
        load.start()
    codes[0] = jnp.zeros((8, NZ), jnp.int32) + ap[0, 0]
    loads[0].wait()
    for t in range(TILES):
        row[1, x, t] = 1.0 / density[t]
    for load in loads[2:]:
        load.start()
    models, images = (bulk_tiles, buoy_tiles), (bulk_image, buoy_image)
    xl, xr, x2 = lax.rem(x + 3, 4), lax.rem(x + 1, 4), lax.rem(x + 2, 4)
    other, same = lax.rem(x + 1, 2), lax.rem(x, 2)
    mine = y * 2 + core
    pending = []

    def start(copy):
        copy.start()
        pending.append(copy)

    def row_copy(f, side, origin):
        part = row.at[f, origin]
        return remote(part, part, x_send.at[0, side, f], x_recv.at[0, side, f], (right, left)[side])

    def half_copy(f, side, origin):
        part = row.at[f, origin, pl.ds(2 * side, 2)]
        return remote(part, part, x_send.at[1, side, f], x_recv.at[1, side, f], (right, left)[side])

    ready()
    for side in range(2):
        start(row_copy(1, side, x))
    for j in range(1, 8):
        start(remote(codes.at[0], codes.at[j], c_send.at[j], c_recv.at[j], ahead[j]))
    loads[1].wait()
    for t in range(TILES):
        fast = speed[t]
        row[0, x, t] = density[t] * fast * fast
    for side in range(2):
        start(row_copy(0, side, x))

    edge = jnp.zeros((PAD, NZ), jnp.float32)
    for ref in (pres, vel0, apres, avel0):
        ref[0:PAD, :] = edge
        ref[PAD + CELLS :, :] = edge
    forward_refs = (pres, vel0, vel1, vel2)
    adjoint_refs = (apres, avel0, avel1, avel2)

    def rows_of(g):
        return pl.ds(g * GROUP, GROUP)

    def padded_of(g):
        return pl.ds(PAD + g * GROUP, GROUP)

    def spots(g):
        return (padded_of(g), padded_of(g), rows_of(g), rows_of(g))

    def unpack(state, refs):
        for g in range(GROUPS):
            for i, (ref, spot) in enumerate(zip(refs, spots(g))):
                ref[spot, :] = state[0, i, rows_of(g), :].astype(jnp.float32)

    def differences(ref, g):
        parts = split(ref[padded_of(g), :])
        return (
            along_x(ref, g * GROUP, 0),
            along_y(yplus[...], parts),
            along_z(parts, zplus[...]),
        )

    def divergence(refs, g):
        return (
            along_x(refs[1], g * GROUP, 1)
            + along_y(yminus[...], split(refs[2][rows_of(g), :]))
            + along_z(split(refs[3][rows_of(g), :]), zminus[...])
        )

    cell = lax.broadcasted_iota(jnp.int32, (NY, NZ), 0) * NZ + lax.broadcasted_iota(jnp.int32, (NY, NZ), 1)
    fired = (src[0, 0] * NY + src[0, 1]) * NZ + src[0, 2]

    def source(n, g):
        planes = []
        for i in range(8):
            planes.append(jnp.where(cell == fired - (g * 8 + i) * NY * NZ, wave[0, n], 0.0))
        return jnp.concatenate(planes, axis=0)

    def received(n, g):
        planes = []
        for i in range(8):
            j = g * 8 + i
            planes.append(jnp.where(cell == recs[0, 0, j] * NZ + recs[0, 1, j], resid[0, n, j], 0.0))
        return jnp.concatenate(planes, axis=0)

    for load in loads[2:]:
        load.wait()
    for state, refs, slot in ((fwd, forward_refs, 0), (adj, adjoint_refs, 1)):
        unpack(state, refs)
        for g in range(GROUPS):
            for d, values in enumerate(differences(refs[0], g)):
                dvel[slot, d, rows_of(g), :] = values

    def select(code, parity, f):
        found = matches(code, parity * 8 + mine)
        chosen = jnp.zeros((8, 8, NZ), jnp.float32)
        for high in range(2):
            for t in range(TILES):
                chosen = jnp.where(found[high][t][None], row[f, parity + 2 * high, t], chosen)
        return chosen

    def tile_copy(parity, own, f, j, origin):
        return remote(
            staged.at[own, f, j], models[f].at[parity * 8 + origin], y_send.at[own, f, j], y_recv.at[own, f, j], back[j]
        )

    def serve(parity, own, f):
        for j in ORDER:
            if own == 0 and f == 1:
                remote(codes.at[0], codes.at[j], c_send.at[j], c_recv.at[j], ahead[j]).wait_recv()
            staged[own, f, j] = select(codes[j], parity, f)
            start(tile_copy(parity, own, f, j, mine))
        models[f][parity * 8 + mine] = select(codes[0], parity, f)

    def arrived(f):
        for own, parity in ((0, other), (1, same)):
            for j in range(1, 8):
                origin = lax.rem(y + j // 2, 4) * 2 + lax.rem(core + j % 2, 2)
                tile_copy(parity, own, f, j, origin).wait_recv()

    for f in (1, 0):
        for side, origin in ((0, xl), (1, xr)):
            row_copy(f, side, origin).wait_recv()
            start(half_copy(f, side, origin))
        serve(other, 0, f)
    for f in (1, 0):
        for side in range(2):
            half_copy(f, side, x2).wait_recv()
        serve(same, 1, f)

    corner = ap[0, 0] >> 2

    def place_model(f, ref):
        for j in range(16):
            values = models[f][(corner + j) & 15]
            ref[pl.ds(j * 2 * NY, 2 * NY), :] = SCALE * values.reshape(2 * NY, NZ)

    arrived(1)
    place_model(1, buoy)
    for g in range(GROUPS):
        light = buoy[rows_of(g), :]
        for d in range(3):
            spot = spots(g)[1 + d]
            change = light * dvel[0, d, rows_of(g), :]
            dvel[0, d, rows_of(g), :] = change
            forward_refs[1 + d][spot, :] += change
            adjoint_refs[1 + d][spot, :] += light * dvel[1, d, rows_of(g), :]
    for g in range(GROUPS):
        dpres[0, rows_of(g), :] = divergence(forward_refs, g)
        dpres[1, rows_of(g), :] = divergence(adjoint_refs, g)
    arrived(0)
    place_model(0, bulk)
    for g in range(GROUPS):
        stiff = bulk[rows_of(g), :]
        change = stiff * dpres[0, rows_of(g), :] + source(0, g)
        dpres[0, rows_of(g), :] = change
        pres[padded_of(g), :] += change
        apres[padded_of(g), :] += stiff * dpres[1, rows_of(g), :] + received(STEPS - 1, g)

    def move(refs, g):
        light = buoy[rows_of(g), :]
        changes, moved = [], []
        for d, values in enumerate(differences(refs[0], g)):
            change = light * values
            after = refs[1 + d][spots(g)[1 + d], :] + change
            refs[1 + d][spots(g)[1 + d], :] = after
            changes.append(change)
            moved.append(after)
        return changes, moved

    def set_image(f, g, values):
        images[f][4 * g : 4 * g + 4] = values.reshape(4, 2 * NY, NZ)

    def get_image(f, g):
        return images[f][4 * g : 4 * g + 4].reshape(GROUP, NZ)

    def inner(changes, others):
        return changes[0] * others[0] + changes[1] * others[1] + changes[2] * others[2]

    def replay(n, carry):
        for g in range(GROUPS):
            changes, _ = move(forward_refs, g)
            for d in range(3):
                dvel[n, d, rows_of(g), :] = changes[d]
        for g in range(GROUPS):
            change = bulk[rows_of(g), :] * divergence(forward_refs, g) + source(n, g)
            dpres[n, rows_of(g), :] = change
            pres[padded_of(g), :] += change
        return carry

    lax.fori_loop(1, STEPS - 1, replay, 0)
    for g in range(GROUPS):
        changes, _ = move(forward_refs, g)
        set_image(1, g, inner(changes, [adjoint_refs[1 + d][spots(g)[1 + d], :] for d in range(3)]))
    for g in range(GROUPS):
        change = bulk[rows_of(g), :] * divergence(forward_refs, g) + source(STEPS - 1, g)
        set_image(0, g, change * apres[padded_of(g), :])

    def adjoint_velocities(n):
        for g in range(GROUPS):
            _, moved = move(adjoint_refs, g)
            set_image(1, g, get_image(1, g) + inner([dvel[n, d, rows_of(g), :] for d in range(3)], moved))

    def adjoint_pressure(n):
        for g in range(GROUPS):
            after = (
                apres[padded_of(g), :]
                + bulk[rows_of(g), :] * divergence(adjoint_refs, g)
                + received(n, g)
            )
            apres[padded_of(g), :] = after
            set_image(0, g, get_image(0, g) + dpres[n, rows_of(g), :] * after)

    def back_step(i, carry):
        adjoint_velocities(STEPS - 2 - i)
        adjoint_pressure(STEPS - 2 - i)
        return carry

    lax.fori_loop(0, STEPS - 2, back_step, 0)

    def image_copy(own, parity, f, h, j):
        target = lax.rem(y + j // 2, 4) * 2 + lax.rem(core + j % 2, 2)
        rows = pl.ds(4 * h, 4)
        return remote(
            image.at[f, parity * 8 + target, rows], came.at[own, f, j, rows],
            iy_send.at[own, f, h, j], iy_recv.at[own, f, h, j], ahead[j],
        )

    def send_image(f):
        for r in range(16):
            image[f, r] = images[f][(r + 16 - corner) & 15].reshape(8, 8, NZ)
        for own, parity in ((1, same), (0, other)):
            for h in range(HALVES):
                for j in ORDER:
                    start(image_copy(own, parity, f, h, j))

    def collect(own, parity, f, h):
        for j in range(1, 8):
            image_copy(own, parity, f, h, j).wait_recv()
        found = [matches(codes[j], parity * 8 + mine) for j in range(8)]
        rows = pl.ds(4 * h, 4)
        for high in range(2):
            for t in range(TILES):
                held = None
                for j in range(8):
                    values = image[f, parity * 8 + mine, rows] if j == 0 else came[own, f, j, rows]
                    term = jnp.where(found[j][high][t][None], values, 0.0)
                    held = term if held is None else held + term
                part[f, h, parity + 2 * high, t] = held

    def hop(stage, side, f, h):
        device, target = ((right, xr), (left, xl))[side]
        if stage == 0:
            origin, landing = part.at[f, h, x2, pl.ds(2 * side, 2)], passed.at[side, f, h]
        else:
            origin, landing = part.at[f, h, target], summed.at[side, f, h]
        return remote(origin, landing, ix_send.at[stage, side, f, h], ix_recv.at[stage, side, f, h], device)

    def collect_same(f, h):
        collect(1, same, f, h)
        for side in range(2):
            start(hop(0, side, f, h))

    def collect_other(f, h):
        collect(0, other, f, h)
        for side, target in ((0, xr), (1, xl)):
            hop(0, side, f, h).wait_recv()
            for i in range(2):
                part[f, h, target, 2 * side + i] += passed[side, f, h, i]
            start(hop(1, side, f, h))

    def piece_copy(f, h, d):
        return remote(
            total.at[f, h, lax.rem(z + d, 8)], terms.at[f, h, d], z_send.at[f, h, d], z_recv.at[f, h, d], column[d]
        )

    outputs = (bulk_sum, buoy_sum)

    def place_of(f, h, piece):
        return outputs[f].at[piece // 2, pl.ds(4 * h + 2 * lax.rem(piece, 2), 2)]

    def result_copy(f, h, d, piece):
        return remote(sums.at[f, h], place_of(f, h, piece), g_send.at[f, h, d], g_recv.at[f, h, d], column[d])

    def keep_copy(f, h):
        return pltpu.make_async_copy(sums.at[f, h], place_of(f, h, z), keep_sems.at[f, h])

    def send_pieces(f, h):
        for side in range(2):
            hop(1, side, f, h).wait_recv()
        for t in range(TILES):
            whole = part[f, h, x, t] + summed[0, f, h, t] + summed[1, f, h, t]
            total[f, h, 2 * t] = whole[:2]
            total[f, h, 2 * t + 1] = whole[2:]
        for d in FAR:
            start(piece_copy(f, h, d))

    def finish_pieces(f, h):
        held = total[f, h, z]
        for d in range(1, 8):
            piece_copy(f, h, d).wait_recv()
            held = held + terms[f, h, d]
        sums[f, h] = held
        keep_copy(f, h).start()
        for d in FAR:
            start(result_copy(f, h, d, z))

    adjoint_velocities(0)
    send_image(1)
    adjoint_pressure(0)
    send_image(0)
    for h in range(HALVES):
        collect_same(1, h)
    for h in range(HALVES):
        collect_other(1, h)
    for h in range(HALVES):
        collect_same(0, h)
        send_pieces(1, h)
    for h in range(HALVES):
        collect_other(0, h)
    for h in range(HALVES):
        send_pieces(0, h)
    for f in (1, 0):
        for h in range(HALVES):
            finish_pieces(f, h)
    for f in (1, 0):
        for h in range(HALVES):
            for d in range(1, 8):
                result_copy(f, h, d, lax.rem(z + 8 - d, 8)).wait_recv()
    for f in range(FIELDS):
        for h in range(HALVES):
            keep_copy(f, h).wait()
    for copy in pending:
        copy.wait_send()


def per_device(speed, density, fwd_state, adj_state, aperture, src_pos, wavelet, rec_pos, residual):
    yplus = difference_matrix(NY, 8)
    zplus = difference_matrix(NZ, 1)
    matrices = [
        jnp.asarray(m, jnp.bfloat16)
        for m in (yplus, -yplus.T, np.concatenate([zplus.T, zplus.T]), np.concatenate([-zplus, -zplus]))
    ]
    smem = pl.BlockSpec(memory_space=pltpu.SMEM)
    whole = pl.BlockSpec(memory_space=pl.ANY)
    dma = pltpu.SemaphoreType.DMA

    def floats(*shape):
        return pltpu.VMEM(shape + (NZ,), jnp.float32)

    def halves(*shape):
        return pltpu.VMEM(shape, jnp.bfloat16)

    tiles = floats(TILES, 8, 8)
    field, wide = floats(CELLS), floats(CELLS + 2 * PAD)
    shape = jax.ShapeDtypeStruct((TILES, 8, 8, NZ), jnp.float32)
    sums = pl.pallas_call(
        kernel,
        out_shape=(shape, shape),
        in_specs=[smem] * 5 + [whole] * 8,
        out_specs=(whole, whole),
        scratch_shapes=[
            tiles, tiles, halves(1, 4, CELLS, NZ), halves(1, 4, CELLS, NZ),
            halves(GROUP, GROUP), halves(GROUP, GROUP), halves(2 * NZ, NZ), halves(2 * NZ, NZ), dma((8,)),
            floats(FIELDS, 4, TILES, 8, 8), floats(2, FIELDS, 8, 8, 8), floats(16, 8, 8), floats(16, 8, 8),
            pltpu.VMEM((8, 8, NZ), jnp.int32),
            dma((2, 2, FIELDS)), dma((2, 2, FIELDS)), dma((8,)), dma((8,)), dma((2, FIELDS, 8)), dma((2, FIELDS, 8)),
            wide, wide, field, field, wide, wide, field, field, field, field,
            floats(STEPS - 1, CELLS), floats(STEPS - 1, 3, CELLS), floats(16, 2 * NY), floats(16, 2 * NY),
            floats(FIELDS, 16, 8, 8), floats(2, FIELDS, 8, 8, 8), floats(FIELDS, HALVES, 4, TILES, 4, 8),
            floats(2, FIELDS, HALVES, 2, 4, 8), floats(2, FIELDS, HALVES, TILES, 4, 8),
            floats(FIELDS, HALVES, 8, 2, 8), floats(FIELDS, HALVES, 8, 2, 8), floats(FIELDS, HALVES, 2, 8),
            dma((2, FIELDS, HALVES, 8)), dma((2, FIELDS, HALVES, 8)),
            dma((2, 2, FIELDS, HALVES)), dma((2, 2, FIELDS, HALVES)),
            dma((FIELDS, HALVES, 8)), dma((FIELDS, HALVES, 8)), dma((FIELDS, HALVES, 8)), dma((FIELDS, HALVES, 8)),
            dma((FIELDS, HALVES)),
        ],
        compiler_params=pltpu.CompilerParams(
            collective_id=0, has_side_effects=True, vmem_limit_bytes=56 * 1024 * 1024
        ),
    )(
        aperture, src_pos, wavelet, rec_pos.transpose(0, 2, 1), residual,
        speed.reshape(TILES, 8, 8, NZ), density.reshape(TILES, 8, 8, NZ),
        fwd_state.reshape(1, 4, CELLS, NZ), adj_state.reshape(1, 4, CELLS, NZ), *matrices,
    )
    bulk_sum, buoy_sum = (values.reshape(speed.shape) for values in sums)
    factor = 1.0 / math.sqrt(lax.axis_size("grp") * lax.axis_size("tile"))
    grad_speed = factor * (bulk_sum * (2.0 * density * speed))
    grad_density = factor * (bulk_sum * (speed * speed) - buoy_sum / (density * density))
    return grad_speed, grad_density


def solution(mesh):
    return jax.shard_map(
        per_device,
        mesh=mesh,
        in_specs=(
            P("tile", None, None, None),
            P("tile", None, None, None),
            P(("grp", "tile"), None, None, None, None),
            P(("grp", "tile"), None, None, None, None),
            P(("grp", "tile"), None),
            P(("grp", "tile"), None),
            P(("grp", "tile"), None),
            P(("grp", "tile"), None, None),
            P(("grp", "tile"), None, None),
        ),
        out_specs=(P("tile", None, None, None), P("tile", None, None, None)),
        check_vma=False,
    )
```
